128 devices in a mesh: space: 64 (over z, y, x_hi, core), spec: 2 (over x_lo).
Axes of the slice: x: 4 (x_hi: 2, x_lo: 2; x = x_hi * 2 + x_lo), y: 4, z: 4, core: 2. Of those that a mesh axis runs over, the one named last changes fastest.
Arguments:
- spectrum: float32 [1296, 256, 512], P('spec', 'space'), may hold values from 0 to 6
- current: float32 [2, 256, 512], P(None, 'space'), may hold values from -4 to 4
- depth: float32 [256, 512], P('space'), may hold values from 8 to 4000
- wind: float32 [2, 256, 512], P(None, 'space'), may hold values from -48 to 48
- sea_blocks: int32 [256, 4], P('space'), may hold values from 0 to 1, as said below
Outputs:
- relaxed: float32 [1296, 256, 512], P('spec', 'space')
The draws below stay inside these ranges and needn't reach their ends.
Inputs may be any that keep to these rules, and one draw needn't show every extreme that they name: `sea_blocks`: each aligned tile of 4 rows holds 1 to 8 sea blocks, and some tile holds exactly 8.
All inputs are finite; a program needn't handle non-finite values.
Results may differ from the reference program's by a relative error of at most 0.0003.
Values sent between devices are 32-bit elements; how exact they have to be, the bound alone decides.
A program may use at most 256 MiB of HBM per device.

```python
import math
import jax
import jax.numpy as jnp
from jax import lax

ND = 36
NF = 36
RX = 4
COLS = 512
BINS = 1296
ROWS = 256
SEA_MAX = 8


def spread_factor(key_dir):
    mean_dir = jax.random.uniform(key_dir, (1, ROWS, COLS), jnp.float32, 0.0, 2.0 * math.pi)
    dir_index = (jnp.arange(BINS, dtype=jnp.int32) // NF).astype(jnp.float32)
    angle = (dir_index * (2.0 * math.pi / ND)).reshape(BINS, 1, 1)
    lobe = jnp.maximum(jnp.cos(angle - mean_dir), 0.0)
    return 0.1 + 0.9 * lobe * lobe


def draw_spectrum(key, part):
    key_base, key_level, key_dir = jax.random.split(key, 3)
    spread = spread_factor(key_dir)
    base_values = jax.random.uniform(key_base, (BINS, ROWS, COLS), jnp.float32, 0.2, 1.0)
    level = jax.random.uniform(key_level, (1, ROWS, COLS), jnp.float32, math.log(0.3), math.log(3.0))
    return base_values * jnp.exp(level) * spread


def tile_order(tile_key):
    return jax.random.permutation(tile_key, RX * (COLS // 128))


def draw_sea_blocks(key, part):
    tile_total = ROWS // RX
    key_count, key_full, key_order = jax.random.split(key, 3)
    counts = jax.random.randint(key_count, (tile_total,), 1, SEA_MAX + 1)
    full_tile = jax.random.randint(key_full, (), 0, tile_total)
    counts = jnp.where(jnp.arange(tile_total) == full_tile, SEA_MAX, counts)
    orders = jax.vmap(tile_order)(jax.random.split(key_order, tile_total))
    ranks = jnp.argsort(orders, axis=1)
    sea_flags = (ranks < counts[:, None]).astype(jnp.int32)
    return sea_flags.reshape(ROWS, COLS // 128)


def shard_levels(rng, shape, pieces, smallest, largest):
    factor_of = 1.0
    for dim, parts in pieces:
        heights = jax.random.uniform(jax.random.fold_in(jax.random.fold_in(rng, 6), dim), (parts,), jnp.float32, smallest / len(pieces), largest / len(pieces))
        factor_of = factor_of * jnp.repeat(jnp.exp(heights), shape[dim] // parts).reshape((-1,) + (1,) * (len(shape) - 1 - dim))
    return factor_of


def noise(key, shape, scale, most, shards=(), kind=jnp.bfloat16):
    factor_of = shard_levels(key, shape, shards, -0.22, 0.18) if shards else 1.0
    array = jax.random.normal(key, shape, jnp.float32) * scale * factor_of
    return jnp.minimum(jnp.maximum(array, -most), most).astype(kind)


def setup_inputs(seed: int = 0) -> dict:
    streams_of = jax.random.split(jax.random.key(seed), 6)
    return {
        "spectrum": draw_spectrum(jax.random.fold_in(streams_of[5], 71), 0),
        "current": noise(streams_of[1], (2, ROWS, COLS), 0.5, 4.0, ((1, 64),), jnp.float32),
        "depth": jnp.clip(jnp.exp(math.log(4000.0) - 6.214608 * jax.random.uniform(streams_of[2], (ROWS, COLS), jnp.float32) ** shard_levels(streams_of[2], (ROWS, COLS), ((0, 64),), -0.2, 0.2)), 8.0, 4000.0),
        "wind": noise(streams_of[3], (2, ROWS, COLS), 8.0, 48.0, ((1, 64),), jnp.float32),
        "sea_blocks": draw_sea_blocks(jax.random.fold_in(streams_of[5], 71), 0),
    }


GRAVITY = 9.81
SIGMA_LOW = 2.0 * math.pi * 0.035
LOG_RATIO = math.log(1.1)
HALF_SPREAD = 0.5 * (1.1 - 1.0 / 1.1)
TIME_STEP = 140.0
CELL_WIDTH = 4600.0
SOURCE_STEP = 280.0
INPUT_COEF = 0.0002
DECAY_COEF = 0.002
STEEP_REF = 600.0
EPSILON = 1e-06

def freq_sigma(freq_index):
    return SIGMA_LOW * jnp.exp(freq_index.astype(jnp.float32) * LOG_RATIO)

def dir_angle(dir_index):
    return dir_index.astype(jnp.float32) * (2.0 * math.pi / ND)

def wavenumber(sigma_freq, depth_cells):
    square = sigma_freq * sigma_freq
    wavenum = square / GRAVITY / jnp.sqrt(jnp.tanh(square * depth_cells / GRAVITY))
    product = wavenum * depth_cells
    damping = jnp.exp(-2.0 * product)
    shallow = 4.0 * product * damping / (1.0 - damping * damping)
    group_speed = 0.5 * (sigma_freq / wavenum) * (1.0 + shallow)
    return (wavenum, group_speed)

def minmod(slope_one, slope_two):
    smaller = jnp.sign(slope_one) * jnp.minimum(jnp.abs(slope_one), jnp.abs(slope_two))
    return jnp.where(slope_one * slope_two > 0.0, smaller, 0.0)

def window(values, offset, length, along_axis):
    return lax.slice_in_dim(values, offset, offset + length, axis=along_axis)

def advect_axis(field_ext, speed_ext, along_axis):
    interior = field_ext.shape[along_axis] - 4
    step_ratio = TIME_STEP / CELL_WIDTH
    differences = window(field_ext, 1, interior + 3, along_axis) - window(field_ext, 0, interior + 3, along_axis)
    face_speed = 0.5 * (window(speed_ext, 1, interior + 1, along_axis) + window(speed_ext, 2, interior + 1, along_axis))
    courant = face_speed * step_ratio
    slope_up = minmod(window(differences, 1, interior + 1, along_axis), window(differences, 0, interior + 1, along_axis))
    slope_down = minmod(window(differences, 2, interior + 1, along_axis), window(differences, 1, interior + 1, along_axis))
    face_up = window(field_ext, 1, interior + 1, along_axis) + 0.5 * (1.0 - courant) * slope_up
    face_down = window(field_ext, 2, interior + 1, along_axis) - 0.5 * (1.0 + courant) * slope_down
    fluxes = face_speed * jnp.where(face_speed >= 0.0, face_up, face_down)
    return window(field_ext, 2, interior, along_axis) - step_ratio * (window(fluxes, 1, interior, along_axis) - window(fluxes, 0, interior, along_axis))

def pad_axis(values, along_axis):
    widths = [(0, 0)] * values.ndim
    widths[along_axis] = (2, 2)
    return jnp.pad(values, widths)

def substep(field_ext, speed_x_ext, speed_y, sea_cells):
    moved_rows = advect_axis(field_ext, speed_x_ext, 1) * sea_cells
    return advect_axis(pad_axis(moved_rows, 2), pad_axis(speed_y, 2), 2) * sea_cells

def source_terms(spectra, depth_cells, wind_x, wind_y):
    ones_tail = (1,) * depth_cells.ndim
    sigma_freq = freq_sigma(jnp.arange(NF, dtype=jnp.int32)).reshape((NF,) + ones_tail)
    direction_angle = dir_angle(jnp.arange(ND, dtype=jnp.int32)).reshape((ND, 1) + ones_tail)
    wavenum, group_unused = wavenumber(sigma_freq, depth_cells[None])
    energy = spectra * (sigma_freq * sigma_freq * HALF_SPREAD * (2.0 * math.pi / ND))
    energy_sum = lax.optimization_barrier(jnp.sum(energy, axis=(0, 1)))
    over_sigma = lax.optimization_barrier(jnp.sum(energy / sigma_freq, axis=(0, 1)))
    over_root = lax.optimization_barrier(jnp.sum(energy / jnp.sqrt(wavenum), axis=(0, 1)))
    mean_sigma = (energy_sum + EPSILON) / (over_sigma + EPSILON)
    mean_wavenum = ((energy_sum + EPSILON) / (over_root + EPSILON)) ** 2
    steepness = energy_sum * mean_wavenum ** 2
    decay_rate = DECAY_COEF * mean_sigma * (wavenum / mean_wavenum) * (steepness / STEEP_REF) ** 2
    wind_along = wind_x * jnp.cos(direction_angle) + wind_y * jnp.sin(direction_angle)
    growth = INPUT_COEF * sigma_freq * jnp.maximum(wind_along * wavenum / sigma_freq - 1.0, 0.0)
    return spectra * (1.0 + SOURCE_STEP * growth) / (1.0 + SOURCE_STEP * decay_rate)

def reference(spectrum, current, depth, wind, sea_blocks):
    sea_cells = jnp.repeat(sea_blocks, 128, axis=1).astype(jnp.float32)
    sigma_freq = freq_sigma(jnp.arange(NF, dtype=jnp.int32)).reshape(NF, 1, 1)
    wavenum, group_speed = wavenumber(sigma_freq, depth[None])
    spectra = spectrum.reshape(ND, NF, ROWS, COLS)

    def propagate(inputs):
        spectra_dir, dir_index = inputs
        direction_angle = dir_angle(dir_index)
        speed_x = group_speed * jnp.cos(direction_angle) + current[0]
        speed_y = group_speed * jnp.sin(direction_angle) + current[1]
        speed_x_ext = pad_axis(speed_x, 1)
        spectra_dir = substep(pad_axis(spectra_dir, 1), speed_x_ext, speed_y, sea_cells)
        spectra_dir = substep(pad_axis(spectra_dir, 1), speed_x_ext, speed_y, sea_cells)
        return spectra_dir
    propagated = lax.map(propagate, (spectra, jnp.arange(ND, dtype=jnp.int32)))
    rows_first = jnp.moveaxis(propagated, 2, 0)

    def relax(inputs):
        spectra_row, depth_row, wind_row = inputs
        return source_terms(spectra_row, depth_row, wind_row[0], wind_row[1])
    relaxed_rows = lax.map(relax, (rows_first, depth, jnp.moveaxis(wind, 1, 0)))
    return jnp.moveaxis(relaxed_rows, 0, 2).reshape(ND * NF, ROWS, COLS)
```

```python
import functools
import math

import jax
import jax.numpy as jnp
import numpy as np
from jax import lax
from jax.experimental import pallas as pl
from jax.experimental.pallas import tpu as pltpu
from jax.sharding import PartitionSpec as P

MESH = pl.DeviceIdType.MESH
ND = 36
NF = 36
GRAVITY = 9.81
SIGMA_LOW = 2.0 * math.pi * 0.035
LOG_RATIO = math.log(1.1)
HALF_SPREAD = 0.5 * (1.1 - 1.0 / 1.1)
STEP_RATIO = 140.0 / 4600.0
SOURCE_STEP = 280.0
INPUT_COEF = 0.0002
DECAY_COEF = 0.002
STEEP_REF = 600.0
EPSILON = 1e-06

LINE = 4
LANES = 128
SLOTS = 8
GROUPS = 81
SLICE = 21
STRIDE = 20
CHUNK = 3
CHUNKS = SLICE // CHUNK
PHASES = 9
TILES = LINE + 2
BLOCKS = 16
CHUNK_ROWS = CHUNK * 8 * BLOCKS
PACK_ROWS = CHUNK * SLOTS * 8
AHEAD = 2


def phase_table(values):
    index = (np.arange(PHASES)[:, None] * 8 + np.arange(8)[None, :]) % NF
    table = values[index].astype(np.float32)
    return np.broadcast_to(table[:, :, None], (PHASES, 8, LANES)).copy()


def sigma_values():
    return SIGMA_LOW * np.exp(np.arange(NF, dtype=np.float64) * LOG_RATIO)


def wide(block):
    return jnp.concatenate([block] * 4, axis=1)


def minmod(a, b):
    return jnp.maximum(jnp.minimum(a, b), 0.0) + jnp.minimum(jnp.maximum(a, b), 0.0)


def face_flux(v, near, far, slope, slope_before, slope_after):
    up = v >= 0.0
    base = jnp.where(up, near, far)
    limited = minmod(slope, jnp.where(up, slope_before, slope_after))
    half = jnp.where(up, 0.5, -0.5) - 0.5 * v
    return v * (base + half * limited)


def wave_number(square, depth):
    return square * (1.0 / GRAVITY) / jnp.sqrt(jnp.tanh(square * depth * (1.0 / GRAVITY)))


def move_kernel(
    lines,
    spectrum,
    fields,
    ids,
    ids_here,
    trig,
    sigma,
    packed_out,
    sums_out,
    arrived,
    field_in,
    ids_in,
    ids_near,
    cg,
    cg_rows,
    cg_cols,
    cur_cols_left,
    cur_rows,
    cur_cols,
    sea,
    moved,
    done,
    packed,
    root,
    sums_mine,
    sums_other,
    in_send,
    in_recv,
    halo_send,
    halo_recv,
    back_send,
    back_recv,
    field_send,
    field_recv,
    fhalo_send,
    fhalo_recv,
    ids_send,
    ids_recv,
    sum_send,
    sum_recv,
    local_sem,
):
    space = lax.axis_index("space")
    half = lax.axis_index("spec")
    other = 1 - half
    line = space // LINE
    place = lax.rem(space, LINE)
    above = (lax.rem(line + lines - 1, lines) * LINE + place, half)
    below = (lax.rem(line + 1, lines) * LINE + place, half)
    members = [(line * LINE + s, other) for s in range(LINE)]

    barrier = pltpu.get_barrier_semaphore()
    for peer in members + [above, below]:
        pl.semaphore_signal(barrier, inc=1, device_id=peer, device_id_type=MESH)
    pl.semaphore_wait(barrier, LINE + 2)

    def remote(src, dst, send, recv, device):
        return pltpu.make_async_remote_copy(
            src_ref=src, dst_ref=dst, send_sem=send, recv_sem=recv, device_id=device, device_id_type=MESH
        )

    def into(k, s, sender):
        start = pl.multiple_of((STRIDE * s * 8 + k * CHUNK * 8) * BLOCKS, 8)
        return remote(
            spectrum.at[pl.ds(start, CHUNK_ROWS)],
            arrived.at[k, 1 + sender],
            in_send.at[k, s],
            in_recv.at[k, sender],
            members[s],
        )

    def halo(k, down):
        tile, target, device = (LINE, 0, below) if down else (1, LINE + 1, above)
        side = 0 if down else 1
        return remote(
            arrived.at[k, tile], arrived.at[k, target], halo_send.at[k, side], halo_recv.at[k, side], device
        )

    def back(k, i, sender):
        return remote(
            packed.at[i, k], packed_out.at[sender, k], back_send.at[k, i], back_recv.at[k, sender], members[i]
        )

    def field_into(s, sender):
        return remote(fields, field_in.at[1 + sender], field_send.at[s], field_recv.at[sender], members[s])

    def ids_into(s, sender):
        return remote(ids, ids_in.at[sender], ids_send.at[s], ids_recv.at[sender], members[s])

    def field_halo(down):
        tile, target, device = (LINE, 0, below) if down else (1, LINE + 1, above)
        side = 0 if down else 1
        return remote(field_in.at[tile], field_in.at[target], fhalo_send.at[side], fhalo_recv.at[side], device)

    for s in range(LINE):
        field_into(s, place).start()
    for s in range(LINE):
        ids_into(s, place).start()
    for k in range(AHEAD):
        for s in range(LINE):
            into(k, s, place).start()

    def root_phase(p, carry):
        square = sigma[p] * sigma[p]
        for slot in range(SLOTS):
            depth = fields[pl.ds(2 * BLOCKS + ids_here[slot], 1), :]
            root[p, slot] = 1.0 / jnp.sqrt(wave_number(square, jnp.broadcast_to(depth, (8, LANES))))
        return carry

    lax.fori_loop(0, PHASES, root_phase, 0)

    for i in range(LINE):
        field_into(i, i).wait_recv()
    field_halo(True).start()
    field_halo(False).start()
    for i in range(LINE):
        ids_into(i, i).wait_recv()
    ids_copy = pltpu.make_async_copy(ids_in, ids_near, local_sem)
    ids_copy.start()
    ids_copy.wait()
    field_halo(True).wait_recv()
    field_halo(False).wait_recv()

    first_line = jnp.where(line == 0, 0.0, 1.0)
    last_line = jnp.where(line == lines - 1, 0.0, 1.0)

    def row_kept(tile):
        return jnp.where(tile == 0, first_line, jnp.where(tile == LINE + 1, last_line, 1.0))

    lane = lax.broadcasted_iota(jnp.int32, (8, 4 * LANES), 1)
    at_start = lane == 0
    at_end = lane == 4 * LANES - 1

    def shift_left(x):
        return jnp.where(at_end, 0.0, pltpu.roll(x, 4 * LANES - 1, 1))

    def field_row(tile, r, which):
        rows = [field_in[tile, pl.ds(which * BLOCKS + ct * 4 + r, 1), :] for ct in range(4)]
        return jnp.broadcast_to(jnp.concatenate(rows, axis=1), (8, 4 * LANES))

    def table_row(row, carry):
        tile, r = row // 4, lax.rem(row, 4)
        kept = row_kept(tile)
        cur_rows[row] = field_row(tile, r, 0) * (0.5 * STEP_RATIO * kept)
        across = field_row(tile, r, 1) * (0.5 * STEP_RATIO * kept)
        cur_cols[row] = across + shift_left(across)
        cur_cols_left[row] = across[:, :LANES]
        sea[row] = field_row(tile, r, 3) * kept
        depth = field_row(tile, r, 2)
        def one_phase(p, inner):
            sig = wide(sigma[p])
            wavenum = wave_number(sig * sig, depth)
            product = wavenum * depth
            damping = jnp.exp(-2.0 * product)
            shallow = 4.0 * product * damping / (1.0 - damping * damping)
            speed = (0.25 * STEP_RATIO * kept) * (sig / wavenum) * (1.0 + shallow)
            cg[row, p] = speed
            cg_cols[row, p] = speed + shift_left(speed)
            return inner
        lax.fori_loop(0, PHASES, one_phase, 0)
        return carry

    lax.fori_loop(0, 4 * TILES, table_row, 0)

    def face_row(row, carry):
        def one_phase(p, inner):
            cg_rows[row, p] = cg[row, p] + cg[row + 1, p]
            return inner
        lax.fori_loop(0, PHASES, one_phase, 0)
        cur_rows[row] = cur_rows[row] + cur_rows[row + 1]
        return carry

    lax.fori_loop(0, 4 * TILES - 1, face_row, 0)

    sub = lax.broadcasted_iota(jnp.int32, (8, 4 * LANES), 0)

    def advance(load, store, first, tiles, phase, cosine, sine):
        def face(row, near, far, slope_before, slope, slope_after):
            v = cg_rows[row, phase] * cosine + cur_rows[row]
            return face_flux(v, near, far, slope, slope_before, slope_after)

        rows = [load(first - 2 + j) for j in range(4)]
        slopes = [rows[j + 1] - rows[j] for j in range(3)]
        flux = face(first - 1, rows[1], rows[2], *slopes)

        def body(t, carry):
            near, far, slope_before, slope, flux_before = carry
            for r in range(4):
                row = first + 4 * t + r
                after = load(row + 2)
                slope_after = after - far
                flux = face(row, near, far, slope_before, slope, slope_after)
                mask = sea[row]
                x = (near - (flux - flux_before)) * mask
                right = shift_left(x)
                d = right - x
                d_before = jnp.where(at_start, x, pltpu.roll(d, 1, 1))
                d_after = shift_left(d)
                v = cg_cols[row, phase] * sine + cur_cols[row]
                across = face_flux(v, x, right, d, d_before, d_after)
                left = cg[row, phase, :, :LANES] * sine[:, :LANES] + cur_cols_left[row]
                x0, d0 = x[:, :LANES], d[:, :LANES]
                first_flux = jnp.minimum(left, 0.0) * (x0 - (0.5 + 0.5 * left) * minmod(d0, x0))
                before = jnp.where(at_start, wide(first_flux), pltpu.roll(across, 1, 1))
                store(t, r, (x - (across - before)) * mask)
                near, far, slope_before, slope, flux_before = far, after, slope, slope_after, flux
            return near, far, slope_before, slope, flux_before

        lax.fori_loop(0, tiles, body, (rows[2], rows[3], slopes[1], slopes[2], flux))

    def compute(k):
        def one_group(m, carry):
            group = STRIDE * place + CHUNK * k + m
            phase = lax.rem(group, PHASES)
            first_bin = other * (8 * GROUPS) + 8 * group
            d, f = first_bin // NF, lax.rem(first_bin, NF)
            later = sub >= NF - f
            cosine = jnp.where(later, trig[0, d + 1], trig[0, d])
            sine = jnp.where(later, trig[1, d + 1], trig[1, d])

            def load_first(row):
                tile, r = row // 4, lax.rem(row, 4)
                parts = [
                    arrived[k, tile, pl.ds(m * 8 * BLOCKS + ct * 4 + r, 8, stride=BLOCKS), :] for ct in range(4)
                ]
                return jnp.concatenate(parts, axis=1) * row_kept(tile)

            def store_first(t, r, value):
                moved[2 + 4 * t + r] = value

            def load_second(row):
                return moved[row]

            def store_second(t, r, value):
                for ct in range(4):
                    done[t * BLOCKS + ct * 4 + r] = value[:, ct * LANES : (ct + 1) * LANES]

            advance(load_first, store_first, 2, LINE + 1, phase, cosine, sine)
            advance(load_second, store_second, 4, LINE, phase, cosine, sine)
            for i in range(LINE):
                for slot in range(SLOTS):
                    packed[i, k, pl.ds((m * SLOTS + slot) * 8, 8), :] = done[i * BLOCKS + ids_near[i, 0, slot]]
            return carry

        lax.fori_loop(0, CHUNK, one_group, 0)

    def step(k, carry):
        @pl.when(k < CHUNKS)
        def _():
            for i in range(LINE):
                into(k, i, i).wait_recv()
            halo(k, True).start()
            halo(k, False).start()
            for s in range(LINE):
                into(k, s, place).wait_send()

        @pl.when(k + AHEAD < CHUNKS)
        def _():
            for s in range(LINE):
                into(k + AHEAD, s, place).start()

        @pl.when(k >= 1)
        def _():
            halo(k - 1, True).wait_recv()
            halo(k - 1, False).wait_recv()
            compute(k - 1)
            for i in range(LINE):
                back(k - 1, i, place).start()

        return carry

    lax.fori_loop(0, CHUNKS + 1, step, 0)

    def finish(k, carry):
        halo(k, True).wait_send()
        halo(k, False).wait_send()
        for i in range(LINE):
            back(k, i, place).wait_send()
        for i in range(LINE):
            back(k, i, i).wait_recv()
        return carry

    lax.fori_loop(0, CHUNKS, finish, 0)
    for s in range(LINE):
        field_into(s, place).wait_send()
        ids_into(s, place).wait_send()
    field_halo(True).wait_send()
    field_halo(False).wait_send()

    totals = [jnp.zeros((8, LANES), jnp.float32)] * (3 * SLOTS)
    for s in range(LINE):
        count = STRIDE if s < LINE - 1 else SLICE

        def add(g, carry, s=s):
            phase = lax.rem(STRIDE * s + g, PHASES)
            chunk, m = g // CHUNK, lax.rem(g, CHUNK)
            sig = sigma[phase]
            weight = sig * sig * (HALF_SPREAD * (2.0 * math.pi / ND))
            over = 1.0 / sig
            result = list(carry)
            for slot in range(SLOTS):
                energy = packed_out[s, chunk, pl.ds((m * SLOTS + slot) * 8, 8), :] * weight
                result[slot] += energy
                result[SLOTS + slot] += energy * over
                result[2 * SLOTS + slot] += energy * root[phase, slot]
            return tuple(result)

        totals = lax.fori_loop(0, count, add, tuple(totals))
    for q in range(3 * SLOTS):
        sums_mine[pl.ds(q, 1), :] = jnp.sum(totals[q], axis=0, keepdims=True)
    swap = remote(sums_mine, sums_other, sum_send, sum_recv, (space, other))
    swap.start()
    swap.wait()
    sums_out[...] = sums_mine[...] + sums_other[...]


def move(lines, spectrum, fields, ids, ids_here, trig, sigma):
    vmem = pl.BlockSpec(memory_space=pltpu.VMEM)
    smem = pl.BlockSpec(memory_space=pltpu.SMEM)
    rows = 4 * TILES
    f32 = jnp.float32
    dma = pltpu.SemaphoreType.DMA
    return pl.pallas_call(
        functools.partial(move_kernel, lines),
        out_shape=(
            jax.ShapeDtypeStruct((LINE, CHUNKS, PACK_ROWS, LANES), f32),
            jax.ShapeDtypeStruct((3 * SLOTS, LANES), f32),
        ),
        in_specs=[pl.BlockSpec(memory_space=pl.ANY), vmem, vmem, smem, smem, vmem],
        out_specs=(vmem, vmem),
        scratch_shapes=[
            pltpu.VMEM((CHUNKS, TILES, CHUNK_ROWS, LANES), f32),
            pltpu.VMEM((TILES, 4 * BLOCKS, LANES), f32),
            pltpu.VMEM((LINE, 8, LANES), jnp.int32),
            pltpu.SMEM((LINE, 8, LANES), jnp.int32),
            pltpu.VMEM((rows, PHASES, 8, 4 * LANES), f32),
            pltpu.VMEM((rows, PHASES, 8, 4 * LANES), f32),
            pltpu.VMEM((rows, PHASES, 8, 4 * LANES), f32),
            pltpu.VMEM((rows, 8, LANES), f32),
            pltpu.VMEM((rows, 8, 4 * LANES), f32),
            pltpu.VMEM((rows, 8, 4 * LANES), f32),
            pltpu.VMEM((rows, 8, 4 * LANES), f32),
            pltpu.VMEM((rows, 8, 4 * LANES), f32),
            pltpu.VMEM((LINE * BLOCKS, 8, LANES), f32),
            pltpu.VMEM((LINE, CHUNKS, PACK_ROWS, LANES), f32),
            pltpu.VMEM((PHASES, SLOTS, 8, LANES), f32),
            pltpu.VMEM((3 * SLOTS, LANES), f32),
            pltpu.VMEM((3 * SLOTS, LANES), f32),
            dma((CHUNKS, LINE)),
            dma((CHUNKS, LINE)),
            dma((CHUNKS, 2)),
            dma((CHUNKS, 2)),
            dma((CHUNKS, LINE)),
            dma((CHUNKS, LINE)),
            dma((LINE,)),
            dma((LINE,)),
            dma((2,)),
            dma((2,)),
            dma((LINE,)),
            dma((LINE,)),
            dma,
            dma,
            dma,
        ],
        compiler_params=pltpu.CompilerParams(
            collective_id=0, has_side_effects=True, vmem_limit_bytes=56 * 1024 * 1024
        ),
        cost_estimate=pl.CostEstimate(flops=250_000_000, bytes_accessed=16_000_000, transcendentals=1_000_000),
    )(spectrum, fields, ids, ids_here, trig, sigma)


def relax_kernel(packed, sums, fields, winds, ids, count, trig, sigma, out, number, brake):
    half = lax.axis_index("spec")
    j = pl.program_id(0)

    @pl.when(j == 0)
    def _():
        def tables(p, carry):
            sig = sigma[p]
            for slot in range(SLOTS):
                depth = jnp.broadcast_to(fields[pl.ds(2 * BLOCKS + ids[slot], 1), :], (8, LANES))
                wavenum = wave_number(sig * sig, depth)
                total = sums[pl.ds(slot, 1), :]
                mean_sigma = (total + EPSILON) / (sums[pl.ds(SLOTS + slot, 1), :] + EPSILON)
                ratio = (total + EPSILON) / (sums[pl.ds(2 * SLOTS + slot, 1), :] + EPSILON)
                mean_wavenum = ratio * ratio
                steep = total * mean_wavenum * mean_wavenum * (1.0 / STEEP_REF)
                rate = (SOURCE_STEP * DECAY_COEF) * mean_sigma * (wavenum / mean_wavenum) * (steep * steep)
                number[p, slot] = wavenum / sig
                brake[p, slot] = 1.0 / (1.0 + rate)
            return carry

        lax.fori_loop(0, PHASES, tables, 0)

    sub = lax.broadcasted_iota(jnp.int32, (8, LANES), 0)
    out[...] = jnp.zeros(out.shape, jnp.float32)
    for q in range(PHASES):
        group = PHASES * j + q
        first_bin = half * (8 * GROUPS) + 8 * group
        d, f = first_bin // NF, lax.rem(first_bin, NF)
        later = sub >= NF - f
        cosine = jnp.where(later, trig[0, d + 1], trig[0, d])
        sine = jnp.where(later, trig[1, d + 1], trig[1, d])
        s = jnp.minimum(group // STRIDE, LINE - 1)
        inside = group - STRIDE * s
        chunk, m = inside // CHUNK, lax.rem(inside, CHUNK)
        gain = sigma[q] * (SOURCE_STEP * INPUT_COEF)
        for slot in range(SLOTS):

            @pl.when(slot < count[0])
            def _(slot=slot):
                blk = ids[slot]
                along = winds[pl.ds(blk, 1), :] * cosine + winds[pl.ds(BLOCKS + blk, 1), :] * sine
                growth = gain * jnp.maximum(along * number[q, slot] - 1.0, 0.0)
                value = packed[s, chunk, pl.ds((m * SLOTS + slot) * 8, 8), :]
                out[pl.ds(q * 8 * BLOCKS + blk, 8, stride=BLOCKS), :] = (
                    value * (1.0 + growth) * brake[q, slot]
                )


def relax(packed, sums, fields, winds, ids, count, trig, sigma):
    vmem = pl.BlockSpec(memory_space=pltpu.VMEM)
    smem = pl.BlockSpec(memory_space=pltpu.SMEM)
    span = PHASES * 8 * BLOCKS
    return pl.pallas_call(
        relax_kernel,
        grid=(GROUPS // PHASES,),
        out_shape=jax.ShapeDtypeStruct((GROUPS * 8 * BLOCKS, LANES), jnp.float32),
        in_specs=[vmem, vmem, vmem, vmem, smem, smem, smem, vmem],
        out_specs=pl.BlockSpec((span, LANES), lambda j: (j, 0)),
        scratch_shapes=[
            pltpu.VMEM((PHASES, SLOTS, 8, LANES), jnp.float32),
            pltpu.VMEM((PHASES, SLOTS, 8, LANES), jnp.float32),
        ],
        compiler_params=pltpu.CompilerParams(vmem_limit_bytes=32 * 1024 * 1024),
        cost_estimate=pl.CostEstimate(flops=7_000_000, bytes_accessed=8_000_000, transcendentals=10_000),
    )(packed, sums, fields, winds, ids, count, trig, sigma)


def tile_rows(array):
    split = array.reshape(array.shape[:-1] + (4, LANES))
    return jnp.swapaxes(split, -3, -2).reshape(-1, LANES)


def on_device(lines, spectrum, current, depth, wind, sea_blocks):
    flags = sea_blocks.T.reshape(BLOCKS)
    rank = jnp.cumsum(flags) - 1
    count = jnp.sum(flags)
    block = jnp.arange(BLOCKS, dtype=jnp.int32)
    slots = jnp.arange(SLOTS, dtype=jnp.int32)
    chosen = (rank[None, :] == slots[:, None]) & (flags[None, :] > 0)
    ids = jnp.sum(jnp.where(chosen, block[None, :], 0), axis=1).astype(jnp.int32)
    ids_wide = jnp.zeros((8, LANES), jnp.int32).at[0, :SLOTS].set(ids)
    mask = jnp.broadcast_to(flags.astype(jnp.float32)[:, None], (BLOCKS, LANES))
    fields = jnp.concatenate([tile_rows(current), tile_rows(depth), mask], axis=0)
    angle = np.arange(ND + 1) * (2.0 * math.pi / ND)
    trig = jnp.asarray(np.stack([np.cos(angle), np.sin(angle)]).astype(np.float32))
    sigma = jnp.asarray(phase_table(sigma_values()))
    packed, sums = move(lines, tile_rows(spectrum), fields, ids_wide, ids, trig, sigma)
    out = relax(packed, sums, fields, tile_rows(wind), ids, count.reshape(1).astype(jnp.int32), trig, sigma)
    return jnp.swapaxes(out.reshape(-1, 4, 4, LANES), 1, 2).reshape(spectrum.shape)


def solution(mesh):
    placed = (
        P("spec", "space", None),
        P(None, "space", None),
        P("space", None),
        P(None, "space", None),
        P("space", None),
    )
    return jax.shard_map(
        functools.partial(on_device, mesh.shape["space"] // LINE),
        mesh=mesh,
        in_specs=placed,
        out_specs=P("spec", "space", None),
        check_vma=False,
    )
```

```python
import functools
import math

import jax
import jax.numpy as jnp
import numpy as np
from jax import lax
from jax.experimental import pallas as pl
from jax.experimental.pallas import tpu as pltpu
from jax.sharding import PartitionSpec as P

MESH = pl.DeviceIdType.MESH
ND = 36
NF = 36
GRAVITY = 9.81
SIGMA_LOW = 2.0 * math.pi * 0.035
LOG_RATIO = math.log(1.1)
HALF_SPREAD = 0.5 * (1.1 - 1.0 / 1.1)
STEP_RATIO = 140.0 / 4600.0
SOURCE_STEP = 280.0
INPUT_COEF = 0.0002
DECAY_COEF = 0.002
STEEP_REF = 600.0
EPSILON = 1e-06

LINE = 4
LANES = 128
SLOTS = 8
GROUPS = 81
SLICE = 20
CHUNKS = ((0, 3), (3, 4), (7, 4), (11, 4), (15, 3), (18, 2), (20, 1))
LAST = len(CHUNKS) - 1
AHEAD = 4
PHASES = 9
TILES = LINE + 2
BLOCKS = 16
GROUP_ROWS = 8 * BLOCKS
PACK_ROWS = 8 * SLOTS
ROWS = 4 * TILES


def phase_tables():
    sigma = SIGMA_LOW * np.exp(np.arange(NF, dtype=np.float64) * LOG_RATIO)
    weight = sigma * sigma * HALF_SPREAD * (2.0 * math.pi / ND)
    index = (np.arange(PHASES)[:, None] * 8 + np.arange(8)[None, :]) % NF
    table = np.stack([sigma, weight, weight / sigma])[:, index].astype(np.float32)
    return np.broadcast_to(table[..., None], table.shape + (LANES,)).copy()


def columns(x):
    return [x[:, ct * LANES : (ct + 1) * LANES] for ct in range(4)]


def each(function, *lists):
    return [function(*parts) for parts in zip(*lists)]


def wave_number(square, depth):
    return square * (1.0 / GRAVITY) / jnp.sqrt(jnp.tanh(square * depth * (1.0 / GRAVITY)))


def face_flux(v, half, near, far, slope, slope_before, slope_after):
    up = v >= 0.0
    other_slope = jnp.where(up, slope_before, slope_after)
    limited = jnp.maximum(jnp.minimum(other_slope, jnp.maximum(slope, 0.0)), jnp.minimum(slope, 0.0))
    return v * (jnp.where(up, near, far) + half * limited)


def half_of(v):
    return jnp.where(v >= 0.0, 0.5, -0.5) - 0.5 * v


def bin_trig(trig, first_bin):
    d, f = first_bin // NF, lax.rem(first_bin, NF)
    later = lax.broadcasted_iota(jnp.int32, (8, LANES), 0) >= NF - f
    return f, jnp.where(later, trig[0, d + 1], trig[0, d]), jnp.where(later, trig[1, d + 1], trig[1, d])


def move_kernel(
    lines,
    spectrum,
    current,
    depth_here,
    flags,
    trig,
    tables,
    packed_out,
    sums_out,
    fields,
    ids,
    ids_here,
    arrived,
    field_in,
    ids_in,
    ids_near,
    cg,
    cg_rows,
    cg_cols,
    cur_rows,
    cur_cols,
    cur_left,
    sea,
    row_v,
    row_half,
    col_v,
    col_half,
    left_v,
    left_half,
    moved,
    done,
    packed,
    returned,
    root,
    sums_mine,
    sums_other,
    in_send,
    in_recv,
    halo_send,
    halo_recv,
    back_send,
    back_recv,
    field_send,
    field_recv,
    fhalo_send,
    fhalo_recv,
    ids_send,
    ids_recv,
    sum_send,
    sum_recv,
    local_sem,
):
    space = lax.axis_index("space")
    half = lax.axis_index("spec")
    other = 1 - half
    line = space // LINE
    place = lax.rem(space, LINE)
    above = (lax.rem(line + lines - 1, lines) * LINE + place, half)
    below = (lax.rem(line + 1, lines) * LINE + place, half)
    members = [(line * LINE + s, other) for s in range(LINE)]
    longer = place == LINE - 1

    barrier = pltpu.get_barrier_semaphore()
    for peer in members + [above, below]:
        pl.semaphore_signal(barrier, inc=1, device_id=peer, device_id_type=MESH)

    lane = lax.broadcasted_iota(jnp.int32, (8, LANES), 1)
    fields[: 2 * BLOCKS] = current[...]
    fields[2 * BLOCKS : 3 * BLOCKS] = depth_here[...]
    numbers = jnp.zeros((8, LANES), jnp.int32)
    found = jnp.int32(0)
    for blk in range(BLOCKS):
        flag = flags[blk % 4, blk // 4]
        fields[3 * BLOCKS + blk : 3 * BLOCKS + blk + 1] = jnp.full((1, LANES), flag.astype(jnp.float32))
        numbers = jnp.where(lane == jnp.where(flag > 0, found, -1), blk, numbers)
        found = found + flag
    ids[...] = numbers
    pl.semaphore_wait(barrier, LINE + 2)

    def remote(src, dst, send, recv, device):
        return pltpu.make_async_remote_copy(
            src_ref=src, dst_ref=dst, send_sem=send, recv_sem=recv, device_id=device, device_id_type=MESH
        )

    def into(c, s, sender):
        first, count = CHUNKS[c]
        return remote(
            spectrum.at[pl.ds((SLICE * s + first) * GROUP_ROWS, count * GROUP_ROWS)],
            arrived.at[1 + sender, pl.ds(first * GROUP_ROWS, count * GROUP_ROWS)],
            in_send.at[c, s],
            in_recv.at[c, sender],
            members[s],
        )

    def halo(c, down):
        first, count = CHUNKS[c]
        part = pl.ds(first * GROUP_ROWS, count * GROUP_ROWS)
        tile, target, device = (LINE, 0, below) if down else (1, LINE + 1, above)
        side = 0 if down else 1
        return remote(
            arrived.at[tile, part], arrived.at[target, part], halo_send.at[c, side], halo_recv.at[c, side], device
        )

    def back(c, i, sender):
        first, count = CHUNKS[c]
        start = pl.multiple_of((SLICE * sender + first) * PACK_ROWS, 8)
        return remote(
            packed.at[i, pl.ds(first * PACK_ROWS, count * PACK_ROWS)],
            returned.at[pl.ds(start, count * PACK_ROWS)],
            back_send.at[c, i],
            back_recv.at[c, sender],
            members[i],
        )

    def field_into(s, sender):
        return remote(fields, field_in.at[1 + sender], field_send.at[s], field_recv.at[sender], members[s])

    def ids_into(s, sender):
        return remote(ids, ids_in.at[sender], ids_send.at[s], ids_recv.at[sender], members[s])

    def field_halo(down):
        tile, target, device = (LINE, 0, below) if down else (1, LINE + 1, above)
        side = 0 if down else 1
        return remote(field_in.at[tile], field_in.at[target], fhalo_send.at[side], fhalo_recv.at[side], device)

    def slices(c):
        return range(LINE) if c < LAST else (LINE - 1,)

    def send_in(c):
        for s in slices(c):
            into(c, s, place).start()

    for s in range(LINE):
        field_into(s, place).start()
    for s in range(LINE):
        ids_into(s, place).start()
    for c in range(AHEAD):
        send_in(c)

    ids_copy = pltpu.make_async_copy(ids, ids_here, local_sem)
    ids_copy.start()
    ids_copy.wait()

    def root_phase(p, carry):
        square = tables[0, p] * tables[0, p]
        for slot in range(SLOTS):
            depth = fields[pl.ds(2 * BLOCKS + ids_here[0, slot], 1), :]
            root[p, slot] = tables[1, p] / jnp.sqrt(wave_number(square, jnp.broadcast_to(depth, (8, LANES))))
        return carry

    lax.fori_loop(0, PHASES, root_phase, 0)

    for i in range(LINE):
        field_into(i, i).wait_recv()
    field_halo(True).start()
    field_halo(False).start()
    for i in range(LINE):
        ids_into(i, i).wait_recv()
    near_copy = pltpu.make_async_copy(ids_in, ids_near, local_sem)
    near_copy.start()
    near_copy.wait()
    field_halo(True).wait_recv()
    field_halo(False).wait_recv()

    first_line = jnp.where(line == 0, 0.0, 1.0)
    last_line = jnp.where(line == lines - 1, 0.0, 1.0)
    at_start = lane == 0
    at_end = lane == LANES - 1

    def shift_left(parts):
        turned = [pltpu.roll(part, LANES - 1, 1) for part in parts] + [jnp.zeros((8, LANES), jnp.float32)]
        return [jnp.where(at_end, turned[ct + 1], turned[ct]) for ct in range(4)]

    def shift_right(parts, first):
        turned = [first] + [pltpu.roll(part, 1, 1) for part in parts]
        return [jnp.where(at_start, turned[ct], turned[ct + 1]) for ct in range(4)]

    def table_row(row, carry):
        tile, r = row // 4, lax.rem(row, 4)
        kept = jnp.where(tile == 0, first_line, jnp.where(tile == LINE + 1, last_line, 1.0))
        scale = 0.5 * STEP_RATIO * kept

        def field_row(which, ct):
            return jnp.broadcast_to(field_in[tile, pl.ds(which * BLOCKS + ct * 4 + r, 1), :], (8, LANES))

        across = [field_row(1, ct) * scale for ct in range(4)]
        cur_left[row] = across[0]
        faces = each(jnp.add, across, shift_left(across))
        for ct in range(4):
            cur_rows[row, ct] = field_row(0, ct) * scale
            cur_cols[row, ct] = faces[ct]
            sea[row, ct] = field_row(3, ct) * kept
        depths = [field_row(2, ct) for ct in range(4)]
        for p in range(5):
            sig = tables[0, p]
            speeds = []
            for ct in range(4):
                wavenum = wave_number(sig * sig, depths[ct])
                product = wavenum * depths[ct]
                damping = jnp.exp(-2.0 * product)
                shallow = 4.0 * product * damping / (1.0 - damping * damping)
                speeds.append((0.5 * scale) * (sig / wavenum) * (1.0 + shallow))
            faces = each(jnp.add, speeds, shift_left(speeds))
            for ct in range(4):
                cg[row, ct, 8 * p : 8 * p + 8] = speeds[ct]
                cg_cols[row, ct, 8 * p : 8 * p + 8] = faces[ct]
        return carry

    def face_row(row, carry):
        cg_rows[row] = cg[row] + cg[row + 1]
        cur_rows[row] = cur_rows[row] + cur_rows[row + 1]
        return carry

    def take_in(c):
        for i in range(LINE):
            into(c, i if c < LAST else LINE - 1, i).wait_recv()
        halo(c, True).start()
        halo(c, False).start()

    def send_more(c):
        for s in slices(c):
            into(c, s, place).wait_send()
        if c + AHEAD < LAST:
            send_in(c + AHEAD)
            if c + AHEAD == LAST - 1:
                send_in(LAST)

    lax.fori_loop(0, ROWS // 2, table_row, 0)
    take_in(0)
    send_more(0)
    lax.fori_loop(ROWS // 2, ROWS, table_row, 0)
    lax.fori_loop(0, ROWS - 1, face_row, 0)

    def advance(load, store, first, tiles, row_speed, col_speed, last_mask):
        rows = [load(first - 2 + j) for j in range(4)]
        slopes = [each(jnp.subtract, rows[j + 1], rows[j]) for j in range(3)]
        flux = each(face_flux, *row_speed(first - 1), rows[1], rows[2], slopes[1], slopes[0], slopes[2])

        def body(t, carry):
            near, far, slope_before, slope, flux_before = carry
            for r in range(4):
                row = first + 4 * t + r
                after = load(row + 2)
                slope_after = each(jnp.subtract, after, far)
                flux = each(face_flux, *row_speed(row), near, far, slope, slope_before, slope_after)
                mask = [sea[row, ct] for ct in range(4)]
                x = each(lambda n, a, b, m: (n - (a - b)) * m, near, flux, flux_before, mask)
                right = shift_left(x)
                d = each(jnp.subtract, right, x)
                v, half_v, edge_v, edge_half = col_speed(row)
                across = each(face_flux, v, half_v, x, right, d, shift_right(d, x[0]), shift_left(d))
                limited = jnp.maximum(jnp.minimum(d[0], jnp.maximum(x[0], 0.0)), jnp.minimum(x[0], 0.0))
                before = shift_right(across, edge_v * (x[0] - edge_half * limited))
                out = each(lambda n, a, b: n - (a - b), x, across, before)
                store(t, r, each(jnp.multiply, out, mask) if last_mask else out)
                near, far, slope_before, slope, flux_before = far, after, slope, slope_after, flux
            return near, far, slope_before, slope, flux_before

        lax.fori_loop(0, tiles, body, (rows[2], rows[3], slopes[1], slopes[2], flux))

    def one_group(group, carry):
        for c in range(1, LAST + 1):
            if c < LAST:

                @pl.when(group == CHUNKS[c - 1][0])
                def _(c=c):
                    take_in(c)
                    send_more(c)

            else:

                @pl.when((group == CHUNKS[c - 1][0]) & longer)
                def _(c=c):
                    take_in(c)

        for c in range(LAST + 1):

            @pl.when(group == CHUNKS[c][0])
            def _(c=c):
                halo(c, True).wait_recv()
                halo(c, False).wait_recv()
                first, count = CHUNKS[c]
                zeros = jnp.zeros((GROUP_ROWS, LANES), jnp.float32)

                @pl.when(line == 0)
                def _():
                    for q in range(count):
                        arrived[0, pl.ds((first + q) * GROUP_ROWS, GROUP_ROWS)] = zeros

                @pl.when(line == lines - 1)
                def _():
                    for q in range(count):
                        arrived[LINE + 1, pl.ds((first + q) * GROUP_ROWS, GROUP_ROWS)] = zeros

        f, cosine, sine = bin_trig(trig, other * (8 * GROUPS) + 8 * (SLICE * place + group))

        def load_first(row):
            tile, r = row // 4, lax.rem(row, 4)
            return [
                arrived[tile, pl.ds(group * GROUP_ROWS + ct * 4 + r, 8, stride=BLOCKS), :] for ct in range(4)
            ]

        def store_first(t, r, value):
            for ct in range(4):
                moved[2 + 4 * t + r, ct] = value[ct]

        def load_second(row):
            return [moved[row, ct] for ct in range(4)]

        def store_second(t, r, value):
            for ct in range(4):
                done[t * BLOCKS + ct * 4 + r] = value[ct]

        def row_first(row):
            v = [cg_rows[row, ct, pl.ds(f, 8), :] * cosine + cur_rows[row, ct] for ct in range(4)]
            halves = each(half_of, v)
            for ct in range(4):
                row_v[row, ct] = v[ct]
                row_half[row, ct] = halves[ct]
            return v, halves

        def col_first(row):
            v = [cg_cols[row, ct, pl.ds(f, 8), :] * sine + cur_cols[row, ct] for ct in range(4)]
            halves = each(half_of, v)
            for ct in range(4):
                col_v[row, ct] = v[ct]
                col_half[row, ct] = halves[ct]
            edge = cg[row, 0, pl.ds(f, 8), :] * sine + cur_left[row]
            edge_v, edge_half = jnp.minimum(edge, 0.0), 0.5 + 0.5 * edge
            left_v[row] = edge_v
            left_half[row] = edge_half
            return v, halves, edge_v, edge_half

        def row_again(row):
            return [row_v[row, ct] for ct in range(4)], [row_half[row, ct] for ct in range(4)]

        def col_again(row):
            v, halves = [col_v[row, ct] for ct in range(4)], [col_half[row, ct] for ct in range(4)]
            return v, halves, left_v[row], left_half[row]

        advance(load_first, store_first, 2, LINE + 1, row_first, col_first, True)
        advance(load_second, store_second, 4, LINE, row_again, col_again, False)
        for i in range(LINE):
            for slot in range(SLOTS):
                start = pl.multiple_of((group * SLOTS + slot) * 8, 8)
                packed[i, pl.ds(start, 8), :] = done[i * BLOCKS + ids_near[i, 0, slot]]

        for c in range(LAST + 1):

            @pl.when(group == CHUNKS[c][0] + CHUNKS[c][1] - 1)
            def _(c=c):
                for i in range(LINE):
                    back(c, i, place).start()

        return carry

    lax.fori_loop(0, jnp.where(longer, SLICE + 1, SLICE), one_group, 0)

    for c in range(LAST + 1):
        for s in slices(c):
            back(c, s, s).wait_recv()

    keep = pltpu.make_async_copy(returned, packed_out, local_sem)
    keep.start()

    def add(g, carry):
        phase = lax.rem(g, PHASES)
        weight, over = tables[1, phase], tables[2, phase]
        result = list(carry)
        for slot in range(SLOTS):
            start = pl.multiple_of((g * SLOTS + slot) * 8, 8)
            value = returned[pl.ds(start, 8), :]
            result[slot] += value * weight
            result[SLOTS + slot] += value * over
            result[2 * SLOTS + slot] += value * root[phase, slot]
        return tuple(result)

    totals = lax.fori_loop(0, GROUPS, add, (jnp.zeros((8, LANES), jnp.float32),) * (3 * SLOTS))
    for q in range(3 * SLOTS):
        sums_mine[pl.ds(q, 1), :] = jnp.sum(totals[q], axis=0, keepdims=True)
    swap = remote(sums_mine, sums_other, sum_send, sum_recv, (space, other))
    swap.start()

    for c in range(LAST):
        halo(c, True).wait_send()
        halo(c, False).wait_send()
        for i in range(LINE):
            back(c, i, place).wait_send()

    @pl.when(longer)
    def _():
        halo(LAST, True).wait_send()
        halo(LAST, False).wait_send()
        for i in range(LINE):
            back(LAST, i, place).wait_send()

    into(LAST, LINE - 1, place).wait_send()
    for s in range(LINE):
        field_into(s, place).wait_send()
        ids_into(s, place).wait_send()
    field_halo(True).wait_send()
    field_halo(False).wait_send()
    keep.wait()
    swap.wait()
    sums_out[...] = sums_mine[...] + sums_other[...]


def move(lines, spectrum, current, depth, flags, trig, tables):
    vmem = pl.BlockSpec(memory_space=pltpu.VMEM)
    smem = pl.BlockSpec(memory_space=pltpu.SMEM)
    hbm = pl.BlockSpec(memory_space=pl.ANY)
    f32 = jnp.float32
    dma = pltpu.SemaphoreType.DMA
    parts = len(CHUNKS)

    def tiles(*shape):
        return pltpu.VMEM(shape + (8, LANES), f32)

    return pl.pallas_call(
        functools.partial(move_kernel, lines),
        out_shape=(
            jax.ShapeDtypeStruct((GROUPS * PACK_ROWS, LANES), f32),
            jax.ShapeDtypeStruct((3 * SLOTS, LANES), f32),
        ),
        in_specs=[hbm, vmem, vmem, smem, smem, vmem],
        out_specs=(hbm, vmem),
        scratch_shapes=[
            pltpu.VMEM((4 * BLOCKS, LANES), f32),
            pltpu.VMEM((8, LANES), jnp.int32),
            pltpu.SMEM((8, LANES), jnp.int32),
            pltpu.VMEM((TILES, (SLICE + 1) * GROUP_ROWS, LANES), f32),
            pltpu.VMEM((TILES, 4 * BLOCKS, LANES), f32),
            pltpu.VMEM((LINE, 8, LANES), jnp.int32),
            pltpu.SMEM((LINE, 8, LANES), jnp.int32),
            pltpu.VMEM((ROWS, 4, 40, LANES), f32),
            pltpu.VMEM((ROWS, 4, 40, LANES), f32),
            pltpu.VMEM((ROWS, 4, 40, LANES), f32),
            tiles(ROWS, 4),
            tiles(ROWS, 4),
            tiles(ROWS),
            tiles(ROWS, 4),
            tiles(ROWS, 4),
            tiles(ROWS, 4),
            tiles(ROWS, 4),
            tiles(ROWS, 4),
            tiles(ROWS),
            tiles(ROWS),
            tiles(ROWS, 4),
            tiles(LINE * BLOCKS),
            pltpu.VMEM((LINE, (SLICE + 1) * PACK_ROWS, LANES), f32),
            pltpu.VMEM((GROUPS * PACK_ROWS, LANES), f32),
            tiles(PHASES, SLOTS),
            pltpu.VMEM((3 * SLOTS, LANES), f32),
            pltpu.VMEM((3 * SLOTS, LANES), f32),
            dma((parts, LINE)),
            dma((parts, LINE)),
            dma((parts, 2)),
            dma((parts, 2)),
            dma((parts, LINE)),
            dma((parts, LINE)),
            dma((LINE,)),
            dma((LINE,)),
            dma((2,)),
            dma((2,)),
            dma((LINE,)),
            dma((LINE,)),
            dma,
            dma,
            dma,
        ],
        compiler_params=pltpu.CompilerParams(
            collective_id=0, has_side_effects=True, vmem_limit_bytes=56 * 1024 * 1024
        ),
        cost_estimate=pl.CostEstimate(flops=250_000_000, bytes_accessed=16_000_000, transcendentals=1_000_000),
    )(spectrum, current, depth, flags, trig, tables)


def relax_kernel(packed, sums, depths, winds, flags, trig, tables, out, ids, gusts, number, brake):
    half = lax.axis_index("spec")
    j = pl.program_id(0)

    @pl.when(j == 0)
    def _():
        total = jnp.int32(0)
        for blk in range(BLOCKS):
            total = total + flags[blk % 4, blk // 4]
        found, dry = jnp.int32(0), total
        for blk in range(BLOCKS):
            flag = flags[blk % 4, blk // 4]
            ids[jnp.where(flag > 0, found, dry)] = blk
            found = found + flag
            dry = dry + 1 - flag
        for slot in range(SLOTS):
            blk = ids[slot]
            gusts[0, slot] = jnp.broadcast_to(winds[pl.ds(blk, 1), :], (8, LANES))
            gusts[1, slot] = jnp.broadcast_to(winds[pl.ds(BLOCKS + blk, 1), :], (8, LANES))
        rates = []
        for slot in range(SLOTS):
            total_here = sums[pl.ds(slot, 1), :]
            mean_sigma = (total_here + EPSILON) / (sums[pl.ds(SLOTS + slot, 1), :] + EPSILON)
            ratio = (total_here + EPSILON) / (sums[pl.ds(2 * SLOTS + slot, 1), :] + EPSILON)
            mean_wavenum = ratio * ratio
            steep = total_here * mean_wavenum * mean_wavenum * (1.0 / STEEP_REF)
            rates.append((SOURCE_STEP * DECAY_COEF) * mean_sigma / mean_wavenum * (steep * steep))

        def fill(p, carry):
            sig = tables[0, p]
            for slot in range(SLOTS):
                depth = jnp.broadcast_to(depths[pl.ds(ids[slot], 1), :], (8, LANES))
                wavenum = wave_number(sig * sig, depth)
                at_sea = jnp.where(slot < total, 1.0, 0.0)
                number[p, slot] = wavenum * (SOURCE_STEP * INPUT_COEF)
                brake[p, slot] = at_sea / (1.0 + rates[slot] * wavenum)
            return carry

        lax.fori_loop(0, PHASES, fill, 0)

    zeros = jnp.zeros((8, LANES), jnp.float32)
    for q in range(PHASES):
        f, cosine, sine = bin_trig(trig, half * (8 * GROUPS) + 8 * (PHASES * j + q))
        gain = tables[0, q] * (SOURCE_STEP * INPUT_COEF)
        for slot in range(SLOTS):
            along = gusts[0, slot] * cosine + gusts[1, slot] * sine
            growth = jnp.maximum(along * number[q, slot] - gain, 0.0)
            value = packed[pl.ds((q * SLOTS + slot) * 8, 8), :]
            out[pl.ds(q * GROUP_ROWS + ids[slot], 8, stride=BLOCKS), :] = value * (1.0 + growth) * brake[q, slot]
        for slot in range(SLOTS, BLOCKS):
            out[pl.ds(q * GROUP_ROWS + ids[slot], 8, stride=BLOCKS), :] = zeros


def relax(packed, sums, depth, wind, flags, trig, tables):
    vmem = pl.BlockSpec(memory_space=pltpu.VMEM)
    smem = pl.BlockSpec(memory_space=pltpu.SMEM)
    f32 = jnp.float32
    return pl.pallas_call(
        relax_kernel,
        grid=(GROUPS // PHASES,),
        out_shape=jax.ShapeDtypeStruct((GROUPS * GROUP_ROWS, LANES), f32),
        in_specs=[pl.BlockSpec((PHASES * PACK_ROWS, LANES), lambda j: (j, 0)), vmem, vmem, vmem, smem, smem, vmem],
        out_specs=pl.BlockSpec((PHASES * GROUP_ROWS, LANES), lambda j: (j, 0)),
        scratch_shapes=[
            pltpu.SMEM((BLOCKS,), jnp.int32),
            pltpu.VMEM((2, SLOTS, 8, LANES), f32),
            pltpu.VMEM((PHASES, SLOTS, 8, LANES), f32),
            pltpu.VMEM((PHASES, SLOTS, 8, LANES), f32),
        ],
        compiler_params=pltpu.CompilerParams(vmem_limit_bytes=32 * 1024 * 1024),
        cost_estimate=pl.CostEstimate(flops=7_000_000, bytes_accessed=8_000_000, transcendentals=10_000),
    )(packed, sums, depth, wind, flags, trig, tables)


def tile_rows(array):
    split = array.reshape(array.shape[:-1] + (4, LANES))
    return jnp.swapaxes(split, -3, -2).reshape(-1, LANES)


def on_device(lines, spectrum, current, depth, wind, sea_blocks):
    angle = np.arange(ND + 1) * (2.0 * math.pi / ND)
    trig = jnp.asarray(np.stack([np.cos(angle), np.sin(angle)]).astype(np.float32))
    tables = jnp.asarray(phase_tables())
    depth_rows = tile_rows(depth)
    packed, sums = move(lines, tile_rows(spectrum), tile_rows(current), depth_rows, sea_blocks, trig, tables)
    out = relax(packed, sums, depth_rows, tile_rows(wind), sea_blocks, trig, tables)
    return jnp.swapaxes(out.reshape(-1, 4, 4, LANES), 1, 2).reshape(spectrum.shape)


def solution(mesh):
    placed = (
        P("spec", "space", None),
        P(None, "space", None),
        P("space", None),
        P(None, "space", None),
        P("space", None),
    )
    return jax.shard_map(
        functools.partial(on_device, mesh.shape["space"] // LINE),
        mesh=mesh,
        in_specs=placed,
        out_specs=P("spec", "space", None),
        check_vma=False,
    )
```

```python
import functools
import math

import jax
import jax.numpy as jnp
import numpy as np
from jax import lax
from jax.experimental import pallas as pl
from jax.experimental.pallas import tpu as pltpu
from jax.sharding import PartitionSpec as P

MESH = pl.DeviceIdType.MESH
ND = 36
NF = 36
GRAVITY = 9.81
SIGMA_LOW = 2.0 * math.pi * 0.035
LOG_RATIO = math.log(1.1)
HALF_SPREAD = 0.5 * (1.1 - 1.0 / 1.1)
STEP_RATIO = 140.0 / 4600.0
SOURCE_STEP = 280.0
INPUT_COEF = 0.0002
DECAY_COEF = 0.002
STEEP_REF = 600.0
EPSILON = 1e-06

LINE = 4
LANES = 128
SLOTS = 8
GROUPS = 81
SLICE = 20
CHUNKS = ((0, 2), (2, 3), (5, 3), (8, 3), (11, 3), (14, 2), (16, 2), (18, 1), (19, 1), (20, 1))
LAST = len(CHUNKS) - 1
EARLY = 4
PHASES = 9
TILES = LINE + 2
BLOCKS = 16
GROUP_ROWS = 8 * BLOCKS
PACK_ROWS = 8 * SLOTS
ROWS = 4 * TILES


def phase_tables():
    sigma = SIGMA_LOW * np.exp(np.arange(NF, dtype=np.float64) * LOG_RATIO)
    weight = sigma * sigma * HALF_SPREAD * (2.0 * math.pi / ND)
    index = (np.arange(PHASES)[:, None] * 8 + np.arange(8)[None, :]) % NF
    table = np.stack([sigma, weight, weight / sigma])[:, index].astype(np.float32)
    return np.broadcast_to(table[..., None], table.shape + (LANES,)).copy()


def columns(x):
    return [x[:, ct * LANES : (ct + 1) * LANES] for ct in range(4)]


def each(function, *lists):
    return [function(*parts) for parts in zip(*lists)]


def wave_number(square, depth):
    return square * (1.0 / GRAVITY) / jnp.sqrt(jnp.tanh(square * depth * (1.0 / GRAVITY)))


def face_flux(v, half, near, far, slope, slope_before, slope_after):
    up = v >= 0.0
    other_slope = jnp.where(up, slope_before, slope_after)
    limited = jnp.maximum(jnp.minimum(other_slope, jnp.maximum(slope, 0.0)), jnp.minimum(slope, 0.0))
    return v * (jnp.where(up, near, far) + half * limited)


def half_of(v):
    return jnp.where(v >= 0.0, 0.5, -0.5) - 0.5 * v


def bin_trig(trig, first_bin):
    d, f = first_bin // NF, lax.rem(first_bin, NF)
    later = lax.broadcasted_iota(jnp.int32, (8, LANES), 0) >= NF - f
    return f, jnp.where(later, trig[0, d + 1], trig[0, d]), jnp.where(later, trig[1, d + 1], trig[1, d])


def move_kernel(
    lines,
    spectrum,
    current,
    depth_here,
    winds,
    flags,
    trig,
    tables,
    packed_out,
    sums_out,
    fields,
    ids,
    ids_here,
    arrived,
    field_in,
    ids_in,
    ids_near,
    cg,
    cg_rows,
    cg_cols,
    cur_rows,
    cur_cols,
    cur_left,
    sea,
    row_v,
    row_half,
    col_v,
    col_half,
    left_v,
    left_half,
    moved,
    done,
    packed,
    returned,
    root,
    number,
    gusts,
    sums_mine,
    sums_other,
    in_send,
    in_recv,
    halo_send,
    halo_recv,
    back_send,
    back_recv,
    field_send,
    field_recv,
    fhalo_send,
    fhalo_recv,
    ids_send,
    ids_recv,
    sum_send,
    sum_recv,
    local_sem,
):
    space = lax.axis_index("space")
    half = lax.axis_index("spec")
    other = 1 - half
    line = space // LINE
    place = lax.rem(space, LINE)
    above = (lax.rem(line + lines - 1, lines) * LINE + place, half)
    below = (lax.rem(line + 1, lines) * LINE + place, half)
    members = [(line * LINE + s, other) for s in range(LINE)]
    longer = place == LINE - 1

    barrier = pltpu.get_barrier_semaphore()
    for peer in members + [above, below]:
        pl.semaphore_signal(barrier, inc=1, device_id=peer, device_id_type=MESH)

    lane = lax.broadcasted_iota(jnp.int32, (8, LANES), 1)
    fields[: 2 * BLOCKS] = current[...]
    fields[2 * BLOCKS : 3 * BLOCKS] = depth_here[...]
    numbers = jnp.zeros((8, LANES), jnp.int32)
    found = jnp.int32(0)
    for blk in range(BLOCKS):
        flag = flags[blk % 4, blk // 4]
        fields[3 * BLOCKS + blk : 3 * BLOCKS + blk + 1] = jnp.full((1, LANES), flag.astype(jnp.float32))
        numbers = jnp.where(lane == jnp.where(flag > 0, found, -1), blk, numbers)
        found = found + flag
    ids[...] = numbers
    pl.semaphore_wait(barrier, LINE + 2)

    def remote(src, dst, send, recv, device):
        return pltpu.make_async_remote_copy(
            src_ref=src, dst_ref=dst, send_sem=send, recv_sem=recv, device_id=device, device_id_type=MESH
        )

    def into(c, s, sender):
        first, count = CHUNKS[c]
        return remote(
            spectrum.at[pl.ds((SLICE * s + first) * GROUP_ROWS, count * GROUP_ROWS)],
            arrived.at[1 + sender, pl.ds(first * GROUP_ROWS, count * GROUP_ROWS)],
            in_send.at[c, s],
            in_recv.at[c, sender],
            members[s],
        )

    def halo(c, down):
        first, count = CHUNKS[c]
        part = pl.ds(first * GROUP_ROWS, count * GROUP_ROWS)
        tile, target, device = (LINE, 0, below) if down else (1, LINE + 1, above)
        side = 0 if down else 1
        return remote(
            arrived.at[tile, part], arrived.at[target, part], halo_send.at[c, side], halo_recv.at[c, side], device
        )

    def back(c, i, sender):
        first, count = CHUNKS[c]
        start = pl.multiple_of((SLICE * sender + first) * PACK_ROWS, 8)
        return remote(
            packed.at[i, pl.ds(first * PACK_ROWS, count * PACK_ROWS)],
            returned.at[pl.ds(start, count * PACK_ROWS)],
            back_send.at[c, i],
            back_recv.at[c, sender],
            members[i],
        )

    def field_into(s, sender):
        return remote(fields, field_in.at[1 + sender], field_send.at[s], field_recv.at[sender], members[s])

    def ids_into(s, sender):
        return remote(ids, ids_in.at[sender], ids_send.at[s], ids_recv.at[sender], members[s])

    def field_halo(down):
        tile, target, device = (LINE, 0, below) if down else (1, LINE + 1, above)
        side = 0 if down else 1
        return remote(field_in.at[tile], field_in.at[target], fhalo_send.at[side], fhalo_recv.at[side], device)

    def slices(c):
        return range(LINE) if c < LAST else (LINE - 1,)

    def send_in(c):
        for s in slices(c):
            into(c, s, place).start()

    for s in range(LINE):
        field_into(s, place).start()
    for s in range(LINE):
        ids_into(s, place).start()
    for c in range(EARLY):
        send_in(c)
    send_in(LAST)
    for c in range(EARLY, LAST):
        send_in(c)

    ids_copy = pltpu.make_async_copy(ids, ids_here, local_sem)
    ids_copy.start()
    ids_copy.wait()

    def root_phase(p, carry):
        square = tables[0, p] * tables[0, p]
        for slot in range(SLOTS):
            depth = fields[pl.ds(2 * BLOCKS + ids_here[0, slot], 1), :]
            wavenum = wave_number(square, jnp.broadcast_to(depth, (8, LANES)))
            root[p, slot] = tables[1, p] / jnp.sqrt(wavenum)
            number[p, slot] = wavenum * (SOURCE_STEP * INPUT_COEF)
        return carry

    for slot in range(SLOTS):
        for part in range(2):
            wind = winds[pl.ds(part * BLOCKS + ids_here[0, slot], 1), :]
            gusts[part, slot] = jnp.broadcast_to(wind, (8, LANES))

    lax.fori_loop(0, PHASES, root_phase, 0)

    for i in range(LINE):
        field_into(i, i).wait_recv()
    field_halo(True).start()
    field_halo(False).start()
    for i in range(LINE):
        ids_into(i, i).wait_recv()
    near_copy = pltpu.make_async_copy(ids_in, ids_near, local_sem)
    near_copy.start()
    near_copy.wait()
    field_halo(True).wait_recv()
    field_halo(False).wait_recv()

    first_line = jnp.where(line == 0, 0.0, 1.0)
    last_line = jnp.where(line == lines - 1, 0.0, 1.0)
    at_start = lane == 0
    at_end = lane == LANES - 1

    def shift_left(parts):
        turned = [pltpu.roll(part, LANES - 1, 1) for part in parts] + [jnp.zeros((8, LANES), jnp.float32)]
        return [jnp.where(at_end, turned[ct + 1], turned[ct]) for ct in range(4)]

    def shift_right(parts, first):
        turned = [first] + [pltpu.roll(part, 1, 1) for part in parts]
        return [jnp.where(at_start, turned[ct], turned[ct + 1]) for ct in range(4)]

    def table_row(row, carry):
        tile, r = row // 4, lax.rem(row, 4)
        kept = jnp.where(tile == 0, first_line, jnp.where(tile == LINE + 1, last_line, 1.0))
        scale = 0.5 * STEP_RATIO * kept

        def field_row(which, ct):
            return jnp.broadcast_to(field_in[tile, pl.ds(which * BLOCKS + ct * 4 + r, 1), :], (8, LANES))

        across = [field_row(1, ct) * scale for ct in range(4)]
        cur_left[row] = across[0]
        faces = each(jnp.add, across, shift_left(across))
        for ct in range(4):
            cur_rows[row, ct] = field_row(0, ct) * scale
            cur_cols[row, ct] = faces[ct]
            sea[row, ct] = field_row(3, ct) * kept
        depths = [field_row(2, ct) for ct in range(4)]
        for p in range(5):
            sig = tables[0, p]
            speeds = []
            for ct in range(4):
                wavenum = wave_number(sig * sig, depths[ct])
                product = wavenum * depths[ct]
                damping = jnp.exp(-2.0 * product)
                shallow = 4.0 * product * damping / (1.0 - damping * damping)
                speeds.append((0.5 * scale) * (sig / wavenum) * (1.0 + shallow))
            faces = each(jnp.add, speeds, shift_left(speeds))
            for ct in range(4):
                cg[row, ct, 8 * p : 8 * p + 8] = speeds[ct]
                cg_cols[row, ct, 8 * p : 8 * p + 8] = faces[ct]
        return carry

    def face_row(row, carry):
        cg_rows[row] = cg[row] + cg[row + 1]
        cur_rows[row] = cur_rows[row] + cur_rows[row + 1]
        return carry

    def take_in(c):
        for i in range(LINE):
            into(c, i if c < LAST else LINE - 1, i).wait_recv()
        halo(c, True).start()
        halo(c, False).start()

    lax.fori_loop(0, ROWS // 2, table_row, 0)
    take_in(0)
    lax.fori_loop(ROWS // 2, ROWS, table_row, 0)
    lax.fori_loop(0, ROWS - 1, face_row, 0)

    def advance(load, store, first, tiles, row_speed, col_speed, last_mask):
        rows = [load(first - 2 + j) for j in range(4)]
        slopes = [each(jnp.subtract, rows[j + 1], rows[j]) for j in range(3)]
        flux = each(face_flux, *row_speed(first - 1), rows[1], rows[2], slopes[1], slopes[0], slopes[2])

        def body(t, carry):
            near, far, slope_before, slope, flux_before = carry
            for r in range(4):
                row = first + 4 * t + r
                after = load(row + 2)
                slope_after = each(jnp.subtract, after, far)
                flux = each(face_flux, *row_speed(row), near, far, slope, slope_before, slope_after)
                mask = [sea[row, ct] for ct in range(4)]
                x = each(lambda n, a, b, m: (n - (a - b)) * m, near, flux, flux_before, mask)
                right = shift_left(x)
                d = each(jnp.subtract, right, x)
                v, half_v, edge_v, edge_half = col_speed(row)
                across = each(face_flux, v, half_v, x, right, d, shift_right(d, x[0]), shift_left(d))
                limited = jnp.maximum(jnp.minimum(d[0], jnp.maximum(x[0], 0.0)), jnp.minimum(x[0], 0.0))
                before = shift_right(across, edge_v * (x[0] - edge_half * limited))
                out = each(lambda n, a, b: n - (a - b), x, across, before)
                store(t, r, each(jnp.multiply, out, mask) if last_mask else out)
                near, far, slope_before, slope, flux_before = far, after, slope, slope_after, flux
            return near, far, slope_before, slope, flux_before

        lax.fori_loop(0, tiles, body, (rows[2], rows[3], slopes[1], slopes[2], flux))

    def one_group(group, carry):
        for c in range(1, LAST + 1):
            if c < LAST:

                @pl.when(group == CHUNKS[c - 1][0])
                def _(c=c):
                    take_in(c)

            else:

                @pl.when((group == CHUNKS[c - 1][0]) & longer)
                def _(c=c):
                    take_in(c)

        for c in range(LAST + 1):

            @pl.when(group == CHUNKS[c][0])
            def _(c=c):
                halo(c, True).wait_recv()
                halo(c, False).wait_recv()
                first, count = CHUNKS[c]
                zeros = jnp.zeros((GROUP_ROWS, LANES), jnp.float32)

                @pl.when(line == 0)
                def _():
                    for q in range(count):
                        arrived[0, pl.ds((first + q) * GROUP_ROWS, GROUP_ROWS)] = zeros

                @pl.when(line == lines - 1)
                def _():
                    for q in range(count):
                        arrived[LINE + 1, pl.ds((first + q) * GROUP_ROWS, GROUP_ROWS)] = zeros

        f, cosine, sine = bin_trig(trig, other * (8 * GROUPS) + 8 * (SLICE * place + group))

        def load_first(row):
            tile, r = row // 4, lax.rem(row, 4)
            return [
                arrived[tile, pl.ds(group * GROUP_ROWS + ct * 4 + r, 8, stride=BLOCKS), :] for ct in range(4)
            ]

        def store_first(t, r, value):
            for ct in range(4):
                moved[2 + 4 * t + r, ct] = value[ct]

        def load_second(row):
            return [moved[row, ct] for ct in range(4)]

        def store_second(t, r, value):
            for ct in range(4):
                done[t * BLOCKS + ct * 4 + r] = value[ct]

        def row_first(row):
            v = [cg_rows[row, ct, pl.ds(f, 8), :] * cosine + cur_rows[row, ct] for ct in range(4)]
            halves = each(half_of, v)
            for ct in range(4):
                row_v[row, ct] = v[ct]
                row_half[row, ct] = halves[ct]
            return v, halves

        def col_first(row):
            v = [cg_cols[row, ct, pl.ds(f, 8), :] * sine + cur_cols[row, ct] for ct in range(4)]
            halves = each(half_of, v)
            for ct in range(4):
                col_v[row, ct] = v[ct]
                col_half[row, ct] = halves[ct]
            edge = cg[row, 0, pl.ds(f, 8), :] * sine + cur_left[row]
            edge_v, edge_half = jnp.minimum(edge, 0.0), 0.5 + 0.5 * edge
            left_v[row] = edge_v
            left_half[row] = edge_half
            return v, halves, edge_v, edge_half

        def row_again(row):
            return [row_v[row, ct] for ct in range(4)], [row_half[row, ct] for ct in range(4)]

        def col_again(row):
            v, halves = [col_v[row, ct] for ct in range(4)], [col_half[row, ct] for ct in range(4)]
            return v, halves, left_v[row], left_half[row]

        advance(load_first, store_first, 2, LINE + 1, row_first, col_first, True)
        advance(load_second, store_second, 4, LINE, row_again, col_again, False)
        for i in range(LINE):
            for slot in range(SLOTS):
                start = pl.multiple_of((group * SLOTS + slot) * 8, 8)
                packed[i, pl.ds(start, 8), :] = done[i * BLOCKS + ids_near[i, 0, slot]]

        for c in range(LAST + 1):

            @pl.when(group == CHUNKS[c][0] + CHUNKS[c][1] - 1)
            def _(c=c):
                for i in range(LINE):
                    back(c, i, place).start()

        return carry

    lax.fori_loop(0, jnp.where(longer, SLICE + 1, SLICE), one_group, 0)

    for s in range(LINE):
        field_into(s, place).wait_send()
        ids_into(s, place).wait_send()
    field_halo(True).wait_send()
    field_halo(False).wait_send()
    for c in range(LAST + 1):
        for s in slices(c):
            into(c, s, place).wait_send()

    totals = (jnp.zeros((8, LANES), jnp.float32),) * (3 * SLOTS)
    for c in (*range(EARLY), LAST, *range(EARLY, LAST)):
        for s in slices(c):
            back(c, s, s).wait_recv()

        def add(m, carry, c=c):
            result = list(carry)
            for s in slices(c):
                g = SLICE * s + m
                phase = lax.rem(g, PHASES)
                weight, over = tables[1, phase], tables[2, phase]
                gain = tables[0, phase] * (SOURCE_STEP * INPUT_COEF)
                _, cosine, sine = bin_trig(trig, half * (8 * GROUPS) + 8 * g)
                for slot in range(SLOTS):
                    start = pl.multiple_of((g * SLOTS + slot) * 8, 8)
                    value = returned[pl.ds(start, 8), :]
                    result[slot] += value * weight
                    result[SLOTS + slot] += value * over
                    result[2 * SLOTS + slot] += value * root[phase, slot]
                    along = gusts[0, slot] * cosine + gusts[1, slot] * sine
                    growth = jnp.maximum(along * number[phase, slot] - gain, 0.0)
                    returned[pl.ds(start, 8), :] = value * (1.0 + growth)
            return tuple(result)

        first, count = CHUNKS[c]
        totals = lax.fori_loop(first, first + count, add, totals)
    keep = pltpu.make_async_copy(returned, packed_out, local_sem)
    keep.start()
    for q in range(3 * SLOTS):
        sums_mine[pl.ds(q, 1), :] = jnp.sum(totals[q], axis=0, keepdims=True)
    swap = remote(sums_mine, sums_other, sum_send, sum_recv, (space, other))
    swap.start()

    for c in range(LAST):
        halo(c, True).wait_send()
        halo(c, False).wait_send()
        for i in range(LINE):
            back(c, i, place).wait_send()

    @pl.when(longer)
    def _():
        halo(LAST, True).wait_send()
        halo(LAST, False).wait_send()
        for i in range(LINE):
            back(LAST, i, place).wait_send()

    keep.wait()
    swap.wait()
    sums_out[...] = sums_mine[...] + sums_other[...]


def move(lines, spectrum, current, depth, wind, flags, trig, tables):
    vmem = pl.BlockSpec(memory_space=pltpu.VMEM)
    smem = pl.BlockSpec(memory_space=pltpu.SMEM)
    hbm = pl.BlockSpec(memory_space=pl.ANY)
    f32 = jnp.float32
    dma = pltpu.SemaphoreType.DMA
    parts = len(CHUNKS)

    def tiles(*shape):
        return pltpu.VMEM(shape + (8, LANES), f32)

    return pl.pallas_call(
        functools.partial(move_kernel, lines),
        out_shape=(
            jax.ShapeDtypeStruct((GROUPS * PACK_ROWS, LANES), f32),
            jax.ShapeDtypeStruct((3 * SLOTS, LANES), f32),
        ),
        in_specs=[hbm, vmem, vmem, vmem, smem, smem, vmem],
        out_specs=(hbm, vmem),
        scratch_shapes=[
            pltpu.VMEM((4 * BLOCKS, LANES), f32),
            pltpu.VMEM((8, LANES), jnp.int32),
            pltpu.SMEM((8, LANES), jnp.int32),
            pltpu.VMEM((TILES, (SLICE + 1) * GROUP_ROWS, LANES), f32),
            pltpu.VMEM((TILES, 4 * BLOCKS, LANES), f32),
            pltpu.VMEM((LINE, 8, LANES), jnp.int32),
            pltpu.SMEM((LINE, 8, LANES), jnp.int32),
            pltpu.VMEM((ROWS, 4, 40, LANES), f32),
            pltpu.VMEM((ROWS, 4, 40, LANES), f32),
            pltpu.VMEM((ROWS, 4, 40, LANES), f32),
            tiles(ROWS, 4),
            tiles(ROWS, 4),
            tiles(ROWS),
            tiles(ROWS, 4),
            tiles(ROWS, 4),
            tiles(ROWS, 4),
            tiles(ROWS, 4),
            tiles(ROWS, 4),
            tiles(ROWS),
            tiles(ROWS),
            tiles(ROWS, 4),
            tiles(LINE * BLOCKS),
            pltpu.VMEM((LINE, (SLICE + 1) * PACK_ROWS, LANES), f32),
            pltpu.VMEM((GROUPS * PACK_ROWS, LANES), f32),
            tiles(PHASES, SLOTS),
            tiles(PHASES, SLOTS),
            tiles(2, SLOTS),
            pltpu.VMEM((3 * SLOTS, LANES), f32),
            pltpu.VMEM((3 * SLOTS, LANES), f32),
            dma((parts, LINE)),
            dma((parts, LINE)),
            dma((parts, 2)),
            dma((parts, 2)),
            dma((parts, LINE)),
            dma((parts, LINE)),
            dma((LINE,)),
            dma((LINE,)),
            dma((2,)),
            dma((2,)),
            dma((LINE,)),
            dma((LINE,)),
            dma,
            dma,
            dma,
        ],
        compiler_params=pltpu.CompilerParams(
            collective_id=0, has_side_effects=True, vmem_limit_bytes=56 * 1024 * 1024
        ),
        cost_estimate=pl.CostEstimate(flops=250_000_000, bytes_accessed=16_000_000, transcendentals=1_000_000),
    )(spectrum, current, depth, wind, flags, trig, tables)


def relax_kernel(packed, sums, depths, flags, tables, out, loaded, ids, brake, staged, in_sems, out_sems):
    span_in, span_out = PHASES * PACK_ROWS, PHASES * GROUP_ROWS
    steps = GROUPS // PHASES

    def copy_in(j):
        part = pl.ds(pl.multiple_of(j * span_in, 8), span_in)
        return pltpu.make_async_copy(packed.at[part], loaded.at[part], in_sems.at[j])

    def copy_out(j):
        here = lax.rem(j, 2)
        part = pl.ds(pl.multiple_of(j * span_out, 8), span_out)
        return pltpu.make_async_copy(staged.at[here], out.at[part], out_sems.at[here])

    for j in range(steps):
        copy_in(j).start()

    total = jnp.int32(0)
    for blk in range(BLOCKS):
        total = total + flags[blk % 4, blk // 4]
    found, dry = jnp.int32(0), total
    for blk in range(BLOCKS):
        flag = flags[blk % 4, blk // 4]
        ids[jnp.where(flag > 0, found, dry)] = blk
        found = found + flag
        dry = dry + 1 - flag
    staged[...] = jnp.zeros(staged.shape, jnp.float32)
    for slot in range(SLOTS):
        here = sums[pl.ds(slot, 1), :]
        mean_sigma = (here + EPSILON) / (sums[pl.ds(SLOTS + slot, 1), :] + EPSILON)
        ratio = (here + EPSILON) / (sums[pl.ds(2 * SLOTS + slot, 1), :] + EPSILON)
        mean_wavenum = ratio * ratio
        steep = here * mean_wavenum * mean_wavenum * (1.0 / STEEP_REF)
        rate = (SOURCE_STEP * DECAY_COEF) * mean_sigma / mean_wavenum * (steep * steep)
        depth = jnp.broadcast_to(depths[pl.ds(ids[slot], 1), :], (8, LANES))
        at_sea = jnp.where(slot < total, 1.0, 0.0)
        for p in range(PHASES):
            wavenum = wave_number(tables[0, p] * tables[0, p], depth)
            brake[p, slot] = at_sea / (1.0 + rate * wavenum)

    def step(j, carry):
        @pl.when(j >= 2)
        def _():
            copy_out(j - 2).wait()

        copy_in(j).wait()
        here = lax.rem(j, 2)
        for q in range(PHASES):
            for slot in range(SLOTS):
                row = pl.multiple_of(j * span_in + (q * SLOTS + slot) * 8, 8)
                place = pl.ds(q * GROUP_ROWS + ids[slot], 8, stride=BLOCKS)
                staged[here, place, :] = loaded[pl.ds(row, 8), :] * brake[q, slot]
        copy_out(j).start()
        return carry

    lax.fori_loop(0, steps, step, 0)
    copy_out(steps - 2).wait()
    copy_out(steps - 1).wait()


def relax(packed, sums, depth, flags, tables):
    vmem = pl.BlockSpec(memory_space=pltpu.VMEM)
    smem = pl.BlockSpec(memory_space=pltpu.SMEM)
    hbm = pl.BlockSpec(memory_space=pl.ANY)
    f32 = jnp.float32
    return pl.pallas_call(
        relax_kernel,
        out_shape=jax.ShapeDtypeStruct((GROUPS * GROUP_ROWS, LANES), f32),
        in_specs=[hbm, vmem, vmem, smem, vmem],
        out_specs=hbm,
        scratch_shapes=[
            pltpu.VMEM((GROUPS * PACK_ROWS, LANES), f32),
            pltpu.SMEM((BLOCKS,), jnp.int32),
            pltpu.VMEM((PHASES, SLOTS, 8, LANES), f32),
            pltpu.VMEM((2, PHASES * GROUP_ROWS, LANES), f32),
            pltpu.SemaphoreType.DMA((GROUPS // PHASES,)),
            pltpu.SemaphoreType.DMA((2,)),
        ],
        compiler_params=pltpu.CompilerParams(vmem_limit_bytes=56 * 1024 * 1024),
        cost_estimate=pl.CostEstimate(flops=1_000_000, bytes_accessed=8_000_000, transcendentals=10_000),
    )(packed, sums, depth, flags, tables)


def tile_rows(array):
    split = array.reshape(array.shape[:-1] + (4, LANES))
    return jnp.swapaxes(split, -3, -2).reshape(-1, LANES)


def on_device(lines, spectrum, current, depth, wind, sea_blocks):
    angle = np.arange(ND + 1) * (2.0 * math.pi / ND)
    trig = jnp.asarray(np.stack([np.cos(angle), np.sin(angle)]).astype(np.float32))
    tables = jnp.asarray(phase_tables())
    depth_rows = tile_rows(depth)
    packed, sums = move(
        lines, tile_rows(spectrum), tile_rows(current), depth_rows, tile_rows(wind), sea_blocks, trig, tables
    )
    out = relax(packed, sums, depth_rows, sea_blocks, tables)
    return jnp.swapaxes(out.reshape(-1, 4, 4, LANES), 1, 2).reshape(spectrum.shape)


def solution(mesh):
    placed = (
        P("spec", "space", None),
        P(None, "space", None),
        P("space", None),
        P(None, "space", None),
        P("space", None),
    )
    return jax.shard_map(
        functools.partial(on_device, mesh.shape["space"] // LINE),
        mesh=mesh,
        in_specs=placed,
        out_specs=P("spec", "space", None),
        check_vma=False,
    )
```

```python
import functools
import math

import jax
import jax.numpy as jnp
import numpy as np
from jax import lax
from jax.experimental import pallas as pl
from jax.experimental.pallas import tpu as pltpu
from jax.sharding import PartitionSpec as P

MESH = pl.DeviceIdType.MESH
ND = 36
NF = 36
GRAVITY = 9.81
SIGMA_LOW = 2.0 * math.pi * 0.035
LOG_RATIO = math.log(1.1)
HALF_SPREAD = 0.5 * (1.1 - 1.0 / 1.1)
STEP_RATIO = 140.0 / 4600.0
SOURCE_STEP = 280.0
INPUT_COEF = 0.0002
DECAY_COEF = 0.002
STEEP_REF = 600.0
EPSILON = 1e-06

LINE = 4
LANES = 128
SLOTS = 8
GROUPS = 81
SLICE = 20
CHUNKS = ((0, 2), (2, 3), (5, 3), (8, 3), (11, 3), (14, 2), (16, 2), (18, 1), (19, 1), (20, 1))
LAST = len(CHUNKS) - 1
EARLY = 4
BUFFERS = 9
PHASES = 9
TILES = LINE + 2
BLOCKS = 16
GROUP_ROWS = 8 * BLOCKS
PACK_ROWS = 8 * SLOTS
ROWS = 4 * TILES


def phase_tables():
    sigma = SIGMA_LOW * np.exp(np.arange(NF, dtype=np.float64) * LOG_RATIO)
    weight = sigma * sigma * HALF_SPREAD * (2.0 * math.pi / ND)
    index = (np.arange(PHASES)[:, None] * 8 + np.arange(8)[None, :]) % NF
    table = np.stack([sigma, weight, weight / sigma])[:, index].astype(np.float32)
    return np.broadcast_to(table[..., None], table.shape + (LANES,)).copy()


def columns(x):
    return [x[:, ct * LANES : (ct + 1) * LANES] for ct in range(4)]


def each(function, *lists):
    return [function(*parts) for parts in zip(*lists)]


def wave_number(square, depth):
    return square * (1.0 / GRAVITY) / jnp.sqrt(jnp.tanh(square * depth * (1.0 / GRAVITY)))


def face_flux(v, half, near, far, slope, slope_before, slope_after):
    up = v >= 0.0
    other_slope = jnp.where(up, slope_before, slope_after)
    limited = jnp.maximum(jnp.minimum(other_slope, jnp.maximum(slope, 0.0)), jnp.minimum(slope, 0.0))
    return v * (jnp.where(up, near, far) + half * limited)


def half_of(v):
    return jnp.where(v >= 0.0, 0.5, -0.5) - 0.5 * v


def bin_trig(trig, first_bin):
    d, f = first_bin // NF, lax.rem(first_bin, NF)
    later = lax.broadcasted_iota(jnp.int32, (8, LANES), 0) >= NF - f
    return f, jnp.where(later, trig[0, d + 1], trig[0, d]), jnp.where(later, trig[1, d + 1], trig[1, d])


def move_kernel(
    lines,
    spectrum,
    current,
    depth_here,
    winds,
    flags,
    trig,
    tables,
    packed_out,
    sums_out,
    fields,
    ids,
    ids_here,
    arrived,
    field_in,
    ids_in,
    ids_near,
    cg,
    cg_rows,
    cg_cols,
    cur_rows,
    cur_cols,
    cur_left,
    sea,
    row_v,
    row_half,
    col_v,
    col_half,
    left_v,
    left_half,
    moved,
    done,
    packed,
    returned,
    root,
    number,
    gusts,
    sums_mine,
    sums_other,
    in_send,
    in_recv,
    halo_send,
    halo_recv,
    back_send,
    back_recv,
    field_send,
    field_recv,
    fhalo_send,
    fhalo_recv,
    ids_send,
    ids_recv,
    sum_send,
    sum_recv,
    keep_sem,
    local_sem,
):
    space = lax.axis_index("space")
    half = lax.axis_index("spec")
    other = 1 - half
    line = space // LINE
    place = lax.rem(space, LINE)
    above = (lax.rem(line + lines - 1, lines) * LINE + place, half)
    below = (lax.rem(line + 1, lines) * LINE + place, half)
    members = [(line * LINE + s, other) for s in range(LINE)]
    longer = place == LINE - 1

    barrier = pltpu.get_barrier_semaphore()
    for peer in members + [above, below]:
        pl.semaphore_signal(barrier, inc=1, device_id=peer, device_id_type=MESH)

    lane = lax.broadcasted_iota(jnp.int32, (8, LANES), 1)
    fields[: 2 * BLOCKS] = current[...]
    fields[2 * BLOCKS : 3 * BLOCKS] = depth_here[...]
    numbers = jnp.zeros((8, LANES), jnp.int32)
    found = jnp.int32(0)
    for blk in range(BLOCKS):
        flag = flags[blk % 4, blk // 4]
        fields[3 * BLOCKS + blk : 3 * BLOCKS + blk + 1] = jnp.full((1, LANES), flag.astype(jnp.float32))
        numbers = jnp.where(lane == jnp.where(flag > 0, found, -1), blk, numbers)
        found = found + flag
    ids[...] = numbers
    pl.semaphore_wait(barrier, LINE + 2)

    def remote(src, dst, send, recv, device):
        return pltpu.make_async_remote_copy(
            src_ref=src, dst_ref=dst, send_sem=send, recv_sem=recv, device_id=device, device_id_type=MESH
        )

    def into(c, s, sender):
        first, count = CHUNKS[c]
        return remote(
            spectrum.at[pl.ds((SLICE * s + first) * GROUP_ROWS, count * GROUP_ROWS)],
            arrived.at[1 + sender, pl.ds(first * GROUP_ROWS, count * GROUP_ROWS)],
            in_send.at[c, s],
            in_recv.at[c, sender],
            members[s],
        )

    def halo(c, down):
        first, count = CHUNKS[c]
        part = pl.ds(first * GROUP_ROWS, count * GROUP_ROWS)
        tile, target, device = (LINE, 0, below) if down else (1, LINE + 1, above)
        side = 0 if down else 1
        return remote(
            arrived.at[tile, part], arrived.at[target, part], halo_send.at[c, side], halo_recv.at[c, side], device
        )

    def back(c, i, sender):
        first, count = CHUNKS[c]
        start = pl.multiple_of((SLICE * sender + first) * PACK_ROWS, 8)
        return remote(
            packed.at[i, pl.ds(first * PACK_ROWS, count * PACK_ROWS)],
            returned.at[pl.ds(start, count * PACK_ROWS)],
            back_send.at[c, i],
            back_recv.at[c, sender],
            members[i],
        )

    def field_into(s, sender):
        return remote(fields, field_in.at[1 + sender], field_send.at[s], field_recv.at[sender], members[s])

    def ids_into(s, sender):
        return remote(ids, ids_in.at[sender], ids_send.at[s], ids_recv.at[sender], members[s])

    def field_halo(down):
        tile, target, device = (LINE, 0, below) if down else (1, LINE + 1, above)
        side = 0 if down else 1
        return remote(field_in.at[tile], field_in.at[target], fhalo_send.at[side], fhalo_recv.at[side], device)

    def slices(c):
        return range(LINE) if c < LAST else (LINE - 1,)

    def send_in(c):
        for s in slices(c):
            into(c, s, place).start()

    for s in range(LINE):
        field_into(s, place).start()
    for s in range(LINE):
        ids_into(s, place).start()
    for c in range(EARLY):
        send_in(c)
    send_in(LAST)
    for c in range(EARLY, LAST):
        send_in(c)

    ids_copy = pltpu.make_async_copy(ids, ids_here, local_sem)
    ids_copy.start()
    ids_copy.wait()

    def root_phase(p, carry):
        square = tables[0, p] * tables[0, p]
        for slot in range(SLOTS):
            depth = fields[pl.ds(2 * BLOCKS + ids_here[0, slot], 1), :]
            wavenum = wave_number(square, jnp.broadcast_to(depth, (8, LANES)))
            root[p, slot] = tables[1, p] / jnp.sqrt(wavenum)
            number[p, slot] = wavenum * (SOURCE_STEP * INPUT_COEF)
        return carry

    for slot in range(SLOTS):
        for part in range(2):
            wind = winds[pl.ds(part * BLOCKS + ids_here[0, slot], 1), :]
            gusts[part, slot] = jnp.broadcast_to(wind, (8, LANES))

    lax.fori_loop(0, PHASES, root_phase, 0)

    for i in range(LINE):
        field_into(i, i).wait_recv()
    field_halo(True).start()
    field_halo(False).start()
    for i in range(LINE):
        ids_into(i, i).wait_recv()
    near_copy = pltpu.make_async_copy(ids_in, ids_near, local_sem)
    near_copy.start()
    near_copy.wait()
    field_halo(True).wait_recv()
    field_halo(False).wait_recv()

    first_line = jnp.where(line == 0, 0.0, 1.0)
    last_line = jnp.where(line == lines - 1, 0.0, 1.0)
    at_start = lane == 0
    at_end = lane == LANES - 1

    def shift_left(parts):
        turned = [pltpu.roll(part, LANES - 1, 1) for part in parts] + [jnp.zeros((8, LANES), jnp.float32)]
        return [jnp.where(at_end, turned[ct + 1], turned[ct]) for ct in range(4)]

    def shift_right(parts, first):
        turned = [first] + [pltpu.roll(part, 1, 1) for part in parts]
        return [jnp.where(at_start, turned[ct], turned[ct + 1]) for ct in range(4)]

    def table_row(row, carry):
        tile, r = row // 4, lax.rem(row, 4)
        kept = jnp.where(tile == 0, first_line, jnp.where(tile == LINE + 1, last_line, 1.0))
        scale = 0.5 * STEP_RATIO * kept

        def field_row(which, ct):
            return jnp.broadcast_to(field_in[tile, pl.ds(which * BLOCKS + ct * 4 + r, 1), :], (8, LANES))

        across = [field_row(1, ct) * scale for ct in range(4)]
        cur_left[row] = across[0]
        faces = each(jnp.add, across, shift_left(across))
        for ct in range(4):
            cur_rows[row, ct] = field_row(0, ct) * scale
            cur_cols[row, ct] = faces[ct]
            sea[row, ct] = field_row(3, ct) * kept
        depths = [field_row(2, ct) for ct in range(4)]
        for p in range(5):
            sig = tables[0, p]
            speeds = []
            for ct in range(4):
                wavenum = wave_number(sig * sig, depths[ct])
                product = wavenum * depths[ct]
                damping = jnp.exp(-2.0 * product)
                shallow = 4.0 * product * damping / (1.0 - damping * damping)
                speeds.append((0.5 * scale) * (sig / wavenum) * (1.0 + shallow))
            faces = each(jnp.add, speeds, shift_left(speeds))
            for ct in range(4):
                cg[row, ct, 8 * p : 8 * p + 8] = speeds[ct]
                cg_cols[row, ct, 8 * p : 8 * p + 8] = faces[ct]
        return carry

    def face_row(row, carry):
        cg_rows[row] = cg[row] + cg[row + 1]
        cur_rows[row] = cur_rows[row] + cur_rows[row + 1]
        return carry

    def take_in(c):
        for i in range(LINE):
            into(c, i if c < LAST else LINE - 1, i).wait_recv()
        halo(c, True).start()
        halo(c, False).start()

    lax.fori_loop(0, ROWS // 2, table_row, 0)
    take_in(0)
    lax.fori_loop(ROWS // 2, ROWS, table_row, 0)
    lax.fori_loop(0, ROWS - 1, face_row, 0)

    def advance(load, store, first, tiles, row_speed, col_speed, last_mask):
        rows = [load(first - 2 + j) for j in range(4)]
        slopes = [each(jnp.subtract, rows[j + 1], rows[j]) for j in range(3)]
        flux = each(face_flux, *row_speed(first - 1), rows[1], rows[2], slopes[1], slopes[0], slopes[2])

        def body(t, carry):
            near, far, slope_before, slope, flux_before = carry
            for r in range(4):
                row = first + 4 * t + r
                after = load(row + 2)
                slope_after = each(jnp.subtract, after, far)
                flux = each(face_flux, *row_speed(row), near, far, slope, slope_before, slope_after)
                mask = [sea[row, ct] for ct in range(4)]
                x = each(lambda n, a, b, m: (n - (a - b)) * m, near, flux, flux_before, mask)
                right = shift_left(x)
                d = each(jnp.subtract, right, x)
                v, half_v, edge_v, edge_half = col_speed(row)
                across = each(face_flux, v, half_v, x, right, d, shift_right(d, x[0]), shift_left(d))
                limited = jnp.maximum(jnp.minimum(d[0], jnp.maximum(x[0], 0.0)), jnp.minimum(x[0], 0.0))
                before = shift_right(across, edge_v * (x[0] - edge_half * limited))
                out = each(lambda n, a, b: n - (a - b), x, across, before)
                store(t, r, each(jnp.multiply, out, mask) if last_mask else out)
                near, far, slope_before, slope, flux_before = far, after, slope, slope_after, flux
            return near, far, slope_before, slope, flux_before

        lax.fori_loop(0, tiles, body, (rows[2], rows[3], slopes[1], slopes[2], flux))

    def one_group(group, carry):
        for c in range(1, LAST + 1):
            if c < LAST:

                @pl.when(group == CHUNKS[c - 1][0])
                def _(c=c):
                    take_in(c)

            else:

                @pl.when((group == CHUNKS[c - 1][0]) & longer)
                def _(c=c):
                    take_in(c)

        for c in range(LAST + 1):

            @pl.when(group == CHUNKS[c][0])
            def _(c=c):
                halo(c, True).wait_recv()
                halo(c, False).wait_recv()
                first, count = CHUNKS[c]
                zeros = jnp.zeros((GROUP_ROWS, LANES), jnp.float32)

                @pl.when(line == 0)
                def _():
                    for q in range(count):
                        arrived[0, pl.ds((first + q) * GROUP_ROWS, GROUP_ROWS)] = zeros

                @pl.when(line == lines - 1)
                def _():
                    for q in range(count):
                        arrived[LINE + 1, pl.ds((first + q) * GROUP_ROWS, GROUP_ROWS)] = zeros

        f, cosine, sine = bin_trig(trig, other * (8 * GROUPS) + 8 * (SLICE * place + group))

        def load_first(row):
            tile, r = row // 4, lax.rem(row, 4)
            return [
                arrived[tile, pl.ds(group * GROUP_ROWS + ct * 4 + r, 8, stride=BLOCKS), :] for ct in range(4)
            ]

        def store_first(t, r, value):
            for ct in range(4):
                moved[2 + 4 * t + r, ct] = value[ct]

        def load_second(row):
            return [moved[row, ct] for ct in range(4)]

        def store_second(t, r, value):
            for ct in range(4):
                done[t * BLOCKS + ct * 4 + r] = value[ct]

        def row_first(row):
            v = [cg_rows[row, ct, pl.ds(f, 8), :] * cosine + cur_rows[row, ct] for ct in range(4)]
            halves = each(half_of, v)
            for ct in range(4):
                row_v[row, ct] = v[ct]
                row_half[row, ct] = halves[ct]
            return v, halves

        def col_first(row):
            v = [cg_cols[row, ct, pl.ds(f, 8), :] * sine + cur_cols[row, ct] for ct in range(4)]
            halves = each(half_of, v)
            for ct in range(4):
                col_v[row, ct] = v[ct]
                col_half[row, ct] = halves[ct]
            edge = cg[row, 0, pl.ds(f, 8), :] * sine + cur_left[row]
            edge_v, edge_half = jnp.minimum(edge, 0.0), 0.5 + 0.5 * edge
            left_v[row] = edge_v
            left_half[row] = edge_half
            return v, halves, edge_v, edge_half

        def row_again(row):
            return [row_v[row, ct] for ct in range(4)], [row_half[row, ct] for ct in range(4)]

        def col_again(row):
            v, halves = [col_v[row, ct] for ct in range(4)], [col_half[row, ct] for ct in range(4)]
            return v, halves, left_v[row], left_half[row]

        advance(load_first, store_first, 2, LINE + 1, row_first, col_first, True)
        advance(load_second, store_second, 4, LINE, row_again, col_again, False)
        for i in range(LINE):
            for slot in range(SLOTS):
                start = pl.multiple_of((group * SLOTS + slot) * 8, 8)
                packed[i, pl.ds(start, 8), :] = done[i * BLOCKS + ids_near[i, 0, slot]]

        for c in range(LAST + 1):

            @pl.when(group == CHUNKS[c][0] + CHUNKS[c][1] - 1)
            def _(c=c):
                for i in range(LINE):
                    back(c, i, place).start()

        return carry

    lax.fori_loop(0, jnp.where(longer, SLICE + 1, SLICE), one_group, 0)

    for s in range(LINE):
        field_into(s, place).wait_send()
        ids_into(s, place).wait_send()
    field_halo(True).wait_send()
    field_halo(False).wait_send()
    for c in range(LAST + 1):
        for s in slices(c):
            into(c, s, place).wait_send()

    split = CHUNKS[LAST - 2][0]

    def keep(late, s):
        begin, end = (split, SLICE + (s == LINE - 1)) if late else (0, split)
        part = pl.ds((SLICE * s + begin) * PACK_ROWS, (end - begin) * PACK_ROWS)
        return pltpu.make_async_copy(returned.at[part], packed_out.at[part], keep_sem.at[late, s])

    totals = (jnp.zeros((8, LANES), jnp.float32),) * (3 * SLOTS)
    for c in (*range(EARLY), LAST, *range(EARLY, LAST)):
        for s in slices(c):
            back(c, s, s).wait_recv()

        def add(m, carry, c=c):
            result = list(carry)
            for s in slices(c):
                g = SLICE * s + m
                phase = lax.rem(g, PHASES)
                weight, over = tables[1, phase], tables[2, phase]
                gain = tables[0, phase] * (SOURCE_STEP * INPUT_COEF)
                _, cosine, sine = bin_trig(trig, half * (8 * GROUPS) + 8 * g)
                for slot in range(SLOTS):
                    start = pl.multiple_of((g * SLOTS + slot) * 8, 8)
                    value = returned[pl.ds(start, 8), :]
                    result[slot] += value * weight
                    result[SLOTS + slot] += value * over
                    result[2 * SLOTS + slot] += value * root[phase, slot]
                    along = gusts[0, slot] * cosine + gusts[1, slot] * sine
                    growth = jnp.maximum(along * number[phase, slot] - gain, 0.0)
                    returned[pl.ds(start, 8), :] = value * (1.0 + growth)
            return tuple(result)

        first, count = CHUNKS[c]
        totals = lax.fori_loop(first, first + count, add, totals)
        if c == LAST - 3:
            for s in range(LINE):
                keep(0, s).start()
    for s in range(LINE):
        keep(1, s).start()
    for q in range(3 * SLOTS):
        sums_mine[pl.ds(q, 1), :] = jnp.sum(totals[q], axis=0, keepdims=True)
    swap = remote(sums_mine, sums_other, sum_send, sum_recv, (space, other))
    swap.start()

    for c in range(LAST):
        halo(c, True).wait_send()
        halo(c, False).wait_send()
        for i in range(LINE):
            back(c, i, place).wait_send()

    @pl.when(longer)
    def _():
        halo(LAST, True).wait_send()
        halo(LAST, False).wait_send()
        for i in range(LINE):
            back(LAST, i, place).wait_send()

    for s in range(LINE):
        keep(0, s).wait()
        keep(1, s).wait()
    swap.wait()
    sums_out[...] = sums_mine[...] + sums_other[...]


def move(lines, spectrum, current, depth, wind, flags, trig, tables):
    vmem = pl.BlockSpec(memory_space=pltpu.VMEM)
    smem = pl.BlockSpec(memory_space=pltpu.SMEM)
    hbm = pl.BlockSpec(memory_space=pl.ANY)
    f32 = jnp.float32
    dma = pltpu.SemaphoreType.DMA
    parts = len(CHUNKS)

    def tiles(*shape):
        return pltpu.VMEM(shape + (8, LANES), f32)

    return pl.pallas_call(
        functools.partial(move_kernel, lines),
        out_shape=(
            jax.ShapeDtypeStruct((GROUPS * PACK_ROWS, LANES), f32),
            jax.ShapeDtypeStruct((3 * SLOTS, LANES), f32),
        ),
        in_specs=[hbm, vmem, vmem, vmem, smem, smem, vmem],
        out_specs=(hbm, vmem),
        scratch_shapes=[
            pltpu.VMEM((4 * BLOCKS, LANES), f32),
            pltpu.VMEM((8, LANES), jnp.int32),
            pltpu.SMEM((8, LANES), jnp.int32),
            pltpu.VMEM((TILES, (SLICE + 1) * GROUP_ROWS, LANES), f32),
            pltpu.VMEM((TILES, 4 * BLOCKS, LANES), f32),
            pltpu.VMEM((LINE, 8, LANES), jnp.int32),
            pltpu.SMEM((LINE, 8, LANES), jnp.int32),
            pltpu.VMEM((ROWS, 4, 40, LANES), f32),
            pltpu.VMEM((ROWS, 4, 40, LANES), f32),
            pltpu.VMEM((ROWS, 4, 40, LANES), f32),
            tiles(ROWS, 4),
            tiles(ROWS, 4),
            tiles(ROWS),
            tiles(ROWS, 4),
            tiles(ROWS, 4),
            tiles(ROWS, 4),
            tiles(ROWS, 4),
            tiles(ROWS, 4),
            tiles(ROWS),
            tiles(ROWS),
            tiles(ROWS, 4),
            tiles(LINE * BLOCKS),
            pltpu.VMEM((LINE, (SLICE + 1) * PACK_ROWS, LANES), f32),
            pltpu.VMEM((GROUPS * PACK_ROWS, LANES), f32),
            tiles(PHASES, SLOTS),
            tiles(PHASES, SLOTS),
            tiles(2, SLOTS),
            pltpu.VMEM((3 * SLOTS, LANES), f32),
            pltpu.VMEM((3 * SLOTS, LANES), f32),
            dma((parts, LINE)),
            dma((parts, LINE)),
            dma((parts, 2)),
            dma((parts, 2)),
            dma((parts, LINE)),
            dma((parts, LINE)),
            dma((LINE,)),
            dma((LINE,)),
            dma((2,)),
            dma((2,)),
            dma((LINE,)),
            dma((LINE,)),
            dma,
            dma,
            dma((2, LINE)),
            dma,
        ],
        compiler_params=pltpu.CompilerParams(
            collective_id=0, has_side_effects=True, vmem_limit_bytes=56 * 1024 * 1024
        ),
        cost_estimate=pl.CostEstimate(flops=250_000_000, bytes_accessed=16_000_000, transcendentals=1_000_000),
    )(spectrum, current, depth, wind, flags, trig, tables)


def relax_kernel(
    packed,
    sums_from,
    depths_from,
    flags_from,
    tables_from,
    out,
    loaded,
    sums,
    depths,
    flags,
    sigma,
    ids,
    brake,
    staged,
    small_sems,
    in_sems,
    out_sems,
):
    span_in, span_out = PHASES * PACK_ROWS, PHASES * GROUP_ROWS
    steps = GROUPS // PHASES

    def copy_in(j):
        part = pl.ds(pl.multiple_of(j * span_in, 8), span_in)
        return pltpu.make_async_copy(packed.at[part], loaded.at[part], in_sems.at[j])

    def copy_out(j):
        here = lax.rem(j, BUFFERS)
        part = pl.ds(pl.multiple_of(j * span_out, 8), span_out)
        return pltpu.make_async_copy(staged.at[here], out.at[part], out_sems.at[here])

    small = [
        pltpu.make_async_copy(flags_from, flags, small_sems.at[0]),
        pltpu.make_async_copy(depths_from, depths, small_sems.at[1]),
        pltpu.make_async_copy(tables_from.at[0], sigma, small_sems.at[2]),
        pltpu.make_async_copy(sums_from, sums, small_sems.at[3]),
    ]
    for copy in small:
        copy.start()
    for j in range(steps):
        copy_in(j).start()
    staged[...] = jnp.zeros(staged.shape, jnp.float32)
    for copy in small:
        copy.wait()

    total = jnp.int32(0)
    for blk in range(BLOCKS):
        total = total + flags[blk % 4, blk // 4]
    found, dry = jnp.int32(0), total
    for blk in range(BLOCKS):
        flag = flags[blk % 4, blk // 4]
        ids[jnp.where(flag > 0, found, dry)] = blk
        found = found + flag
        dry = dry + 1 - flag
    for slot in range(SLOTS):
        here = sums[pl.ds(slot, 1), :]
        mean_sigma = (here + EPSILON) / (sums[pl.ds(SLOTS + slot, 1), :] + EPSILON)
        ratio = (here + EPSILON) / (sums[pl.ds(2 * SLOTS + slot, 1), :] + EPSILON)
        mean_wavenum = ratio * ratio
        steep = here * mean_wavenum * mean_wavenum * (1.0 / STEEP_REF)
        rate = (SOURCE_STEP * DECAY_COEF) * mean_sigma / mean_wavenum * (steep * steep)
        depth = jnp.broadcast_to(depths[pl.ds(ids[slot], 1), :], (8, LANES))
        at_sea = jnp.where(slot < total, 1.0, 0.0)
        for p in range(PHASES):
            wavenum = wave_number(sigma[p] * sigma[p], depth)
            brake[p, slot] = at_sea / (1.0 + rate * wavenum)

    def step(j, carry):
        if BUFFERS < steps:

            @pl.when(j >= BUFFERS)
            def _():
                copy_out(j - BUFFERS).wait()

        copy_in(j).wait()
        here = lax.rem(j, BUFFERS)
        for q in range(PHASES):
            for slot in range(SLOTS):
                row = pl.multiple_of(j * span_in + (q * SLOTS + slot) * 8, 8)
                place = pl.ds(q * GROUP_ROWS + ids[slot], 8, stride=BLOCKS)
                staged[here, place, :] = loaded[pl.ds(row, 8), :] * brake[q, slot]
        copy_out(j).start()
        return carry

    lax.fori_loop(0, steps, step, 0)
    for j in range(steps - BUFFERS, steps):
        copy_out(j).wait()


def relax(packed, sums, depth, flags, tables):
    hbm = pl.BlockSpec(memory_space=pl.ANY)
    f32 = jnp.float32
    return pl.pallas_call(
        relax_kernel,
        out_shape=jax.ShapeDtypeStruct((GROUPS * GROUP_ROWS, LANES), f32),
        in_specs=[hbm] * 5,
        out_specs=hbm,
        scratch_shapes=[
            pltpu.VMEM((GROUPS * PACK_ROWS, LANES), f32),
            pltpu.VMEM((3 * SLOTS, LANES), f32),
            pltpu.VMEM((BLOCKS, LANES), f32),
            pltpu.SMEM((4, 4), jnp.int32),
            pltpu.VMEM((PHASES, 8, LANES), f32),
            pltpu.SMEM((BLOCKS,), jnp.int32),
            pltpu.VMEM((PHASES, SLOTS, 8, LANES), f32),
            pltpu.VMEM((BUFFERS, PHASES * GROUP_ROWS, LANES), f32),
            pltpu.SemaphoreType.DMA((4,)),
            pltpu.SemaphoreType.DMA((GROUPS // PHASES,)),
            pltpu.SemaphoreType.DMA((BUFFERS,)),
        ],
        compiler_params=pltpu.CompilerParams(vmem_limit_bytes=56 * 1024 * 1024),
        cost_estimate=pl.CostEstimate(flops=1_000_000, bytes_accessed=8_000_000, transcendentals=10_000),
    )(packed, sums, depth, flags, tables)


def tile_rows(array):
    split = array.reshape(array.shape[:-1] + (4, LANES))
    return jnp.swapaxes(split, -3, -2).reshape(-1, LANES)


def on_device(lines, spectrum, current, depth, wind, sea_blocks):
    angle = np.arange(ND + 1) * (2.0 * math.pi / ND)
    trig = jnp.asarray(np.stack([np.cos(angle), np.sin(angle)]).astype(np.float32))
    tables = jnp.asarray(phase_tables())
    depth_rows = tile_rows(depth)
    packed, sums = move(
        lines, tile_rows(spectrum), tile_rows(current), depth_rows, tile_rows(wind), sea_blocks, trig, tables
    )
    out = relax(packed, sums, depth_rows, sea_blocks, tables)
    return jnp.swapaxes(out.reshape(-1, 4, 4, LANES), 1, 2).reshape(spectrum.shape)


def solution(mesh):
    placed = (
        P("spec", "space", None),
        P(None, "space", None),
        P("space", None),
        P(None, "space", None),
        P("space", None),
    )
    return jax.shard_map(
        functools.partial(on_device, mesh.shape["space"] // LINE),
        mesh=mesh,
        in_specs=placed,
        out_specs=P("spec", "space", None),
        check_vma=False,
    )
```

```python
import functools
import math

import jax
import jax.numpy as jnp
import numpy as np
from jax import lax
from jax.experimental import pallas as pl
from jax.experimental.pallas import tpu as pltpu
from jax.sharding import PartitionSpec as P

MESH = pl.DeviceIdType.MESH
ND = 36
NF = 36
GRAVITY = 9.81
SIGMA_LOW = 2.0 * math.pi * 0.035
LOG_RATIO = math.log(1.1)
HALF_SPREAD = 0.5 * (1.1 - 1.0 / 1.1)
STEP_RATIO = 140.0 / 4600.0
SOURCE_STEP = 280.0
INPUT_COEF = 0.0002
DECAY_COEF = 0.002
STEEP_REF = 600.0
EPSILON = 1e-06

LINE = 4
LANES = 128
SLOTS = 8
GROUPS = 81
SLICE = 20
CHUNKS = ((0, 2), (2, 3), (5, 3), (8, 3), (11, 3), (14, 2), (16, 2), (18, 1), (19, 1), (20, 1))
LAST = len(CHUNKS) - 1
EARLY = 4
BUFFERS = 9
PHASES = 9
TILES = LINE + 2
BLOCKS = 16
GROUP_ROWS = 8 * BLOCKS
PACK_ROWS = 8 * SLOTS
ROWS = 4 * TILES


def phase_tables():
    sigma = SIGMA_LOW * np.exp(np.arange(NF, dtype=np.float64) * LOG_RATIO)
    weight = sigma * sigma * HALF_SPREAD * (2.0 * math.pi / ND)
    index = (np.arange(PHASES)[:, None] * 8 + np.arange(8)[None, :]) % NF
    table = np.stack([sigma, weight, weight / sigma])[:, index].astype(np.float32)
    return np.broadcast_to(table[..., None], table.shape + (LANES,)).copy()


def columns(x):
    return [x[:, ct * LANES : (ct + 1) * LANES] for ct in range(4)]


def each(function, *lists):
    return [function(*parts) for parts in zip(*lists)]


def wave_number(square, depth):
    return square * (1.0 / GRAVITY) / jnp.sqrt(jnp.tanh(square * depth * (1.0 / GRAVITY)))


def face_flux(v, half, near, far, slope, slope_before, slope_after):
    up = v >= 0.0
    other_slope = jnp.where(up, slope_before, slope_after)
    limited = jnp.maximum(jnp.minimum(other_slope, jnp.maximum(slope, 0.0)), jnp.minimum(slope, 0.0))
    return v * (jnp.where(up, near, far) + half * limited)


def half_of(v):
    return jnp.where(v >= 0.0, 0.5, -0.5) - 0.5 * v


def bin_trig(trig, first_bin):
    d, f = first_bin // NF, lax.rem(first_bin, NF)
    later = lax.broadcasted_iota(jnp.int32, (8, LANES), 0) >= NF - f
    return f, jnp.where(later, trig[0, d + 1], trig[0, d]), jnp.where(later, trig[1, d + 1], trig[1, d])


def move_kernel(
    lines,
    spectrum,
    current_from,
    depth_from,
    winds_from,
    flags_from,
    trig_from,
    tables_from,
    packed_out,
    sums_out,
    winds,
    flags,
    trig,
    tables,
    fields,
    ids,
    ids_here,
    arrived,
    field_in,
    ids_in,
    ids_near,
    cg,
    cg_rows,
    cg_cols,
    cur_rows,
    cur_cols,
    cur_left,
    sea,
    row_v,
    row_half,
    col_v,
    col_half,
    left_v,
    left_half,
    moved,
    done,
    packed,
    returned,
    root,
    number,
    gusts,
    sums_mine,
    sums_other,
    in_send,
    in_recv,
    halo_send,
    halo_recv,
    back_send,
    back_recv,
    field_send,
    field_recv,
    fhalo_send,
    fhalo_recv,
    ids_send,
    ids_recv,
    sum_send,
    sum_recv,
    keep_sem,
    small_sem,
    local_sem,
):
    space = lax.axis_index("space")
    half = lax.axis_index("spec")
    other = 1 - half
    line = space // LINE
    place = lax.rem(space, LINE)
    above = (lax.rem(line + lines - 1, lines) * LINE + place, half)
    below = (lax.rem(line + 1, lines) * LINE + place, half)
    members = [(line * LINE + s, other) for s in range(LINE)]
    longer = place == LINE - 1

    barrier = pltpu.get_barrier_semaphore()
    for peer in members + [above, below]:
        pl.semaphore_signal(barrier, inc=1, device_id=peer, device_id_type=MESH)

    small = [
        pltpu.make_async_copy(flags_from, flags, small_sem.at[0]),
        pltpu.make_async_copy(current_from, fields.at[pl.ds(0, 2 * BLOCKS)], small_sem.at[1]),
        pltpu.make_async_copy(depth_from, fields.at[pl.ds(2 * BLOCKS, BLOCKS)], small_sem.at[2]),
        pltpu.make_async_copy(tables_from, tables, small_sem.at[3]),
        pltpu.make_async_copy(winds_from, winds, small_sem.at[4]),
        pltpu.make_async_copy(trig_from, trig, small_sem.at[5]),
    ]
    for copy in small:
        copy.start()
    for copy in small:
        copy.wait()

    lane = lax.broadcasted_iota(jnp.int32, (8, LANES), 1)
    numbers = jnp.zeros((8, LANES), jnp.int32)
    found = jnp.int32(0)
    for blk in range(BLOCKS):
        flag = flags[blk % 4, blk // 4]
        fields[3 * BLOCKS + blk : 3 * BLOCKS + blk + 1] = jnp.full((1, LANES), flag.astype(jnp.float32))
        numbers = jnp.where(lane == jnp.where(flag > 0, found, -1), blk, numbers)
        found = found + flag
    ids[...] = numbers
    pl.semaphore_wait(barrier, LINE + 2)

    def remote(src, dst, send, recv, device):
        return pltpu.make_async_remote_copy(
            src_ref=src, dst_ref=dst, send_sem=send, recv_sem=recv, device_id=device, device_id_type=MESH
        )

    def into(c, s, sender):
        first, count = CHUNKS[c]
        return remote(
            spectrum.at[pl.ds((SLICE * s + first) * GROUP_ROWS, count * GROUP_ROWS)],
            arrived.at[1 + sender, pl.ds(first * GROUP_ROWS, count * GROUP_ROWS)],
            in_send.at[c, s],
            in_recv.at[c, sender],
            members[s],
        )

    def halo(c, down):
        first, count = CHUNKS[c]
        part = pl.ds(first * GROUP_ROWS, count * GROUP_ROWS)
        tile, target, device = (LINE, 0, below) if down else (1, LINE + 1, above)
        side = 0 if down else 1
        return remote(
            arrived.at[tile, part], arrived.at[target, part], halo_send.at[c, side], halo_recv.at[c, side], device
        )

    def back(c, i, sender):
        first, count = CHUNKS[c]
        start = pl.multiple_of((SLICE * sender + first) * PACK_ROWS, 8)
        return remote(
            packed.at[i, pl.ds(first * PACK_ROWS, count * PACK_ROWS)],
            returned.at[pl.ds(start, count * PACK_ROWS)],
            back_send.at[c, i],
            back_recv.at[c, sender],
            members[i],
        )

    def field_into(s, sender):
        return remote(fields, field_in.at[1 + sender], field_send.at[s], field_recv.at[sender], members[s])

    def ids_into(s, sender):
        return remote(ids, ids_in.at[sender], ids_send.at[s], ids_recv.at[sender], members[s])

    def field_halo(down):
        tile, target, device = (LINE, 0, below) if down else (1, LINE + 1, above)
        side = 0 if down else 1
        return remote(field_in.at[tile], field_in.at[target], fhalo_send.at[side], fhalo_recv.at[side], device)

    def slices(c):
        return range(LINE) if c < LAST else (LINE - 1,)

    def send_in(c):
        for s in slices(c):
            into(c, s, place).start()

    for s in range(LINE):
        field_into(s, place).start()
    for s in range(LINE):
        ids_into(s, place).start()
    for c in range(EARLY):
        send_in(c)
    send_in(LAST)
    for c in range(EARLY, LAST):
        send_in(c)

    ids_copy = pltpu.make_async_copy(ids, ids_here, local_sem)
    ids_copy.start()
    ids_copy.wait()

    def root_phase(p, carry):
        square = tables[0, p] * tables[0, p]
        for slot in range(SLOTS):
            depth = fields[pl.ds(2 * BLOCKS + ids_here[0, slot], 1), :]
            wavenum = wave_number(square, jnp.broadcast_to(depth, (8, LANES)))
            root[p, slot] = tables[1, p] / jnp.sqrt(wavenum)
            number[p, slot] = wavenum * (SOURCE_STEP * INPUT_COEF)
        return carry

    for slot in range(SLOTS):
        for part in range(2):
            wind = winds[pl.ds(part * BLOCKS + ids_here[0, slot], 1), :]
            gusts[part, slot] = jnp.broadcast_to(wind, (8, LANES))

    lax.fori_loop(0, PHASES, root_phase, 0)

    for i in range(LINE):
        field_into(i, i).wait_recv()
    field_halo(True).start()
    field_halo(False).start()
    for i in range(LINE):
        ids_into(i, i).wait_recv()
    near_copy = pltpu.make_async_copy(ids_in, ids_near, local_sem)
    near_copy.start()
    near_copy.wait()
    field_halo(True).wait_recv()
    field_halo(False).wait_recv()

    first_line = jnp.where(line == 0, 0.0, 1.0)
    last_line = jnp.where(line == lines - 1, 0.0, 1.0)
    at_start = lane == 0
    at_end = lane == LANES - 1

    def shift_left(parts):
        turned = [pltpu.roll(part, LANES - 1, 1) for part in parts] + [jnp.zeros((8, LANES), jnp.float32)]
        return [jnp.where(at_end, turned[ct + 1], turned[ct]) for ct in range(4)]

    def shift_right(parts, first):
        turned = [first] + [pltpu.roll(part, 1, 1) for part in parts]
        return [jnp.where(at_start, turned[ct], turned[ct + 1]) for ct in range(4)]

    def table_row(row, carry):
        tile, r = row // 4, lax.rem(row, 4)
        kept = jnp.where(tile == 0, first_line, jnp.where(tile == LINE + 1, last_line, 1.0))
        scale = 0.5 * STEP_RATIO * kept

        def field_row(which, ct):
            return jnp.broadcast_to(field_in[tile, pl.ds(which * BLOCKS + ct * 4 + r, 1), :], (8, LANES))

        across = [field_row(1, ct) * scale for ct in range(4)]
        cur_left[row] = across[0]
        faces = each(jnp.add, across, shift_left(across))
        for ct in range(4):
            cur_rows[row, ct] = field_row(0, ct) * scale
            cur_cols[row, ct] = faces[ct]
            sea[row, ct] = field_row(3, ct) * kept
        depths = [field_row(2, ct) for ct in range(4)]
        for p in range(5):
            sig = tables[0, p]
            speeds = []
            for ct in range(4):
                wavenum = wave_number(sig * sig, depths[ct])
                product = wavenum * depths[ct]
                damping = jnp.exp(-2.0 * product)
                shallow = 4.0 * product * damping / (1.0 - damping * damping)
                speeds.append((0.5 * scale) * (sig / wavenum) * (1.0 + shallow))
            faces = each(jnp.add, speeds, shift_left(speeds))
            for ct in range(4):
                cg[row, ct, 8 * p : 8 * p + 8] = speeds[ct]
                cg_cols[row, ct, 8 * p : 8 * p + 8] = faces[ct]
        return carry

    def face_row(row, carry):
        cg_rows[row] = cg[row] + cg[row + 1]
        cur_rows[row] = cur_rows[row] + cur_rows[row + 1]
        return carry

    def take_in(c):
        for i in range(LINE):
            into(c, i if c < LAST else LINE - 1, i).wait_recv()
        halo(c, True).start()
        halo(c, False).start()

    lax.fori_loop(0, ROWS // 2, table_row, 0)
    take_in(0)
    lax.fori_loop(ROWS // 2, ROWS, table_row, 0)
    lax.fori_loop(0, ROWS - 1, face_row, 0)

    def advance(load, store, first, tiles, row_speed, col_speed, last_mask):
        rows = [load(first - 2 + j) for j in range(4)]
        slopes = [each(jnp.subtract, rows[j + 1], rows[j]) for j in range(3)]
        flux = each(face_flux, *row_speed(first - 1), rows[1], rows[2], slopes[1], slopes[0], slopes[2])

        def body(t, carry):
            near, far, slope_before, slope, flux_before = carry
            for r in range(4):
                row = first + 4 * t + r
                after = load(row + 2)
                slope_after = each(jnp.subtract, after, far)
                flux = each(face_flux, *row_speed(row), near, far, slope, slope_before, slope_after)
                mask = [sea[row, ct] for ct in range(4)]
                x = each(lambda n, a, b, m: (n - (a - b)) * m, near, flux, flux_before, mask)
                right = shift_left(x)
                d = each(jnp.subtract, right, x)
                v, half_v, edge_v, edge_half = col_speed(row)
                across = each(face_flux, v, half_v, x, right, d, shift_right(d, x[0]), shift_left(d))
                limited = jnp.maximum(jnp.minimum(d[0], jnp.maximum(x[0], 0.0)), jnp.minimum(x[0], 0.0))
                before = shift_right(across, edge_v * (x[0] - edge_half * limited))
                out = each(lambda n, a, b: n - (a - b), x, across, before)
                store(t, r, each(jnp.multiply, out, mask) if last_mask else out)
                near, far, slope_before, slope, flux_before = far, after, slope, slope_after, flux
            return near, far, slope_before, slope, flux_before

        lax.fori_loop(0, tiles, body, (rows[2], rows[3], slopes[1], slopes[2], flux))

    def one_group(group, carry):
        for c in range(1, LAST + 1):
            if c < LAST:

                @pl.when(group == CHUNKS[c - 1][0])
                def _(c=c):
                    take_in(c)

            else:

                @pl.when((group == CHUNKS[c - 1][0]) & longer)
                def _(c=c):
                    take_in(c)

        for c in range(LAST + 1):

            @pl.when(group == CHUNKS[c][0])
            def _(c=c):
                halo(c, True).wait_recv()
                halo(c, False).wait_recv()
                first, count = CHUNKS[c]
                zeros = jnp.zeros((GROUP_ROWS, LANES), jnp.float32)

                @pl.when(line == 0)
                def _():
                    for q in range(count):
                        arrived[0, pl.ds((first + q) * GROUP_ROWS, GROUP_ROWS)] = zeros

                @pl.when(line == lines - 1)
                def _():
                    for q in range(count):
                        arrived[LINE + 1, pl.ds((first + q) * GROUP_ROWS, GROUP_ROWS)] = zeros

        f, cosine, sine = bin_trig(trig, other * (8 * GROUPS) + 8 * (SLICE * place + group))

        def load_first(row):
            tile, r = row // 4, lax.rem(row, 4)
            return [
                arrived[tile, pl.ds(group * GROUP_ROWS + ct * 4 + r, 8, stride=BLOCKS), :] for ct in range(4)
            ]

        def store_first(t, r, value):
            for ct in range(4):
                moved[2 + 4 * t + r, ct] = value[ct]

        def load_second(row):
            return [moved[row, ct] for ct in range(4)]

        def store_second(t, r, value):
            for ct in range(4):
                done[t * BLOCKS + ct * 4 + r] = value[ct]

        def row_first(row):
            v = [cg_rows[row, ct, pl.ds(f, 8), :] * cosine + cur_rows[row, ct] for ct in range(4)]
            halves = each(half_of, v)
            for ct in range(4):
                row_v[row, ct] = v[ct]
                row_half[row, ct] = halves[ct]
            return v, halves

        def col_first(row):
            v = [cg_cols[row, ct, pl.ds(f, 8), :] * sine + cur_cols[row, ct] for ct in range(4)]
            halves = each(half_of, v)
            for ct in range(4):
                col_v[row, ct] = v[ct]
                col_half[row, ct] = halves[ct]
            edge = cg[row, 0, pl.ds(f, 8), :] * sine + cur_left[row]
            edge_v, edge_half = jnp.minimum(edge, 0.0), 0.5 + 0.5 * edge
            left_v[row] = edge_v
            left_half[row] = edge_half
            return v, halves, edge_v, edge_half

        def row_again(row):
            return [row_v[row, ct] for ct in range(4)], [row_half[row, ct] for ct in range(4)]

        def col_again(row):
            v, halves = [col_v[row, ct] for ct in range(4)], [col_half[row, ct] for ct in range(4)]
            return v, halves, left_v[row], left_half[row]

        advance(load_first, store_first, 2, LINE + 1, row_first, col_first, True)
        advance(load_second, store_second, 4, LINE, row_again, col_again, False)
        for i in range(LINE):
            for slot in range(SLOTS):
                start = pl.multiple_of((group * SLOTS + slot) * 8, 8)
                packed[i, pl.ds(start, 8), :] = done[i * BLOCKS + ids_near[i, 0, slot]]

        for c in range(LAST + 1):

            @pl.when(group == CHUNKS[c][0] + CHUNKS[c][1] - 1)
            def _(c=c):
                for i in range(LINE):
                    back(c, i, place).start()

        return carry

    lax.fori_loop(0, jnp.where(longer, SLICE + 1, SLICE), one_group, 0)

    for s in range(LINE):
        field_into(s, place).wait_send()
        ids_into(s, place).wait_send()
    field_halo(True).wait_send()
    field_halo(False).wait_send()
    for c in range(LAST + 1):
        for s in slices(c):
            into(c, s, place).wait_send()

    split = CHUNKS[LAST - 2][0]

    def keep(late, s):
        begin, end = (split, SLICE + (s == LINE - 1)) if late else (0, split)
        part = pl.ds((SLICE * s + begin) * PACK_ROWS, (end - begin) * PACK_ROWS)
        return pltpu.make_async_copy(returned.at[part], packed_out.at[part], keep_sem.at[late, s])

    totals = (jnp.zeros((8, LANES), jnp.float32),) * (3 * SLOTS)
    for c in (*range(EARLY), LAST, *range(EARLY, LAST)):
        for s in slices(c):
            back(c, s, s).wait_recv()

        def add(m, carry, c=c):
            result = list(carry)
            for s in slices(c):
                g = SLICE * s + m
                phase = lax.rem(g, PHASES)
                weight, over = tables[1, phase], tables[2, phase]
                gain = tables[0, phase] * (SOURCE_STEP * INPUT_COEF)
                _, cosine, sine = bin_trig(trig, half * (8 * GROUPS) + 8 * g)
                for slot in range(SLOTS):
                    start = pl.multiple_of((g * SLOTS + slot) * 8, 8)
                    value = returned[pl.ds(start, 8), :]
                    result[slot] += value * weight
                    result[SLOTS + slot] += value * over
                    result[2 * SLOTS + slot] += value * root[phase, slot]
                    along = gusts[0, slot] * cosine + gusts[1, slot] * sine
                    growth = jnp.maximum(along * number[phase, slot] - gain, 0.0)
                    returned[pl.ds(start, 8), :] = value * (1.0 + growth)
            return tuple(result)

        first, count = CHUNKS[c]
        totals = lax.fori_loop(first, first + count, add, totals)
        if c == LAST - 3:
            for s in range(LINE):
                keep(0, s).start()
    for s in range(LINE):
        keep(1, s).start()
    for q in range(3 * SLOTS):
        sums_mine[pl.ds(q, 1), :] = jnp.sum(totals[q], axis=0, keepdims=True)
    swap = remote(sums_mine, sums_other, sum_send, sum_recv, (space, other))
    swap.start()

    for c in range(LAST):
        halo(c, True).wait_send()
        halo(c, False).wait_send()
        for i in range(LINE):
            back(c, i, place).wait_send()

    @pl.when(longer)
    def _():
        halo(LAST, True).wait_send()
        halo(LAST, False).wait_send()
        for i in range(LINE):
            back(LAST, i, place).wait_send()

    for s in range(LINE):
        keep(0, s).wait()
        keep(1, s).wait()
    swap.wait()
    sums_out[...] = sums_mine[...] + sums_other[...]


def move(lines, spectrum, current, depth, wind, flags, trig, tables):
    vmem = pl.BlockSpec(memory_space=pltpu.VMEM)
    hbm = pl.BlockSpec(memory_space=pl.ANY)
    f32 = jnp.float32
    dma = pltpu.SemaphoreType.DMA
    parts = len(CHUNKS)

    def tiles(*shape):
        return pltpu.VMEM(shape + (8, LANES), f32)

    return pl.pallas_call(
        functools.partial(move_kernel, lines),
        out_shape=(
            jax.ShapeDtypeStruct((GROUPS * PACK_ROWS, LANES), f32),
            jax.ShapeDtypeStruct((3 * SLOTS, LANES), f32),
        ),
        in_specs=[hbm] * 7,
        out_specs=(hbm, vmem),
        scratch_shapes=[
            pltpu.VMEM((2 * BLOCKS, LANES), f32),
            pltpu.SMEM((4, 4), jnp.int32),
            pltpu.SMEM((2, ND + 1), f32),
            tiles(3, PHASES),
            pltpu.VMEM((4 * BLOCKS, LANES), f32),
            pltpu.VMEM((8, LANES), jnp.int32),
            pltpu.SMEM((8, LANES), jnp.int32),
            pltpu.VMEM((TILES, (SLICE + 1) * GROUP_ROWS, LANES), f32),
            pltpu.VMEM((TILES, 4 * BLOCKS, LANES), f32),
            pltpu.VMEM((LINE, 8, LANES), jnp.int32),
            pltpu.SMEM((LINE, 8, LANES), jnp.int32),
            pltpu.VMEM((ROWS, 4, 40, LANES), f32),
            pltpu.VMEM((ROWS, 4, 40, LANES), f32),
            pltpu.VMEM((ROWS, 4, 40, LANES), f32),
            tiles(ROWS, 4),
            tiles(ROWS, 4),
            tiles(ROWS),
            tiles(ROWS, 4),
            tiles(ROWS, 4),
            tiles(ROWS, 4),
            tiles(ROWS, 4),
            tiles(ROWS, 4),
            tiles(ROWS),
            tiles(ROWS),
            tiles(ROWS, 4),
            tiles(LINE * BLOCKS),
            pltpu.VMEM((LINE, (SLICE + 1) * PACK_ROWS, LANES), f32),
            pltpu.VMEM((GROUPS * PACK_ROWS, LANES), f32),
            tiles(PHASES, SLOTS),
            tiles(PHASES, SLOTS),
            tiles(2, SLOTS),
            pltpu.VMEM((3 * SLOTS, LANES), f32),
            pltpu.VMEM((3 * SLOTS, LANES), f32),
            dma((parts, LINE)),
            dma((parts, LINE)),
            dma((parts, 2)),
            dma((parts, 2)),
            dma((parts, LINE)),
            dma((parts, LINE)),
            dma((LINE,)),
            dma((LINE,)),
            dma((2,)),
            dma((2,)),
            dma((LINE,)),
            dma((LINE,)),
            dma,
            dma,
            dma((2, LINE)),
            dma((6,)),
            dma,
        ],
        compiler_params=pltpu.CompilerParams(
            collective_id=0, has_side_effects=True, vmem_limit_bytes=56 * 1024 * 1024
        ),
        cost_estimate=pl.CostEstimate(flops=250_000_000, bytes_accessed=16_000_000, transcendentals=1_000_000),
    )(spectrum, current, depth, wind, flags, trig, tables)


def relax_kernel(
    packed,
    sums_from,
    depths_from,
    flags_from,
    tables_from,
    out,
    loaded,
    sums,
    depths,
    flags,
    sigma,
    ids,
    brake,
    staged,
    small_sems,
    in_sems,
    out_sems,
):
    span_in, span_out = PHASES * PACK_ROWS, PHASES * GROUP_ROWS
    steps = GROUPS // PHASES

    def copy_in(j):
        part = pl.ds(pl.multiple_of(j * span_in, 8), span_in)
        return pltpu.make_async_copy(packed.at[part], loaded.at[part], in_sems.at[j])

    def copy_out(j):
        here = lax.rem(j, BUFFERS)
        part = pl.ds(pl.multiple_of(j * span_out, 8), span_out)
        return pltpu.make_async_copy(staged.at[here], out.at[part], out_sems.at[here])

    small = [
        pltpu.make_async_copy(flags_from, flags, small_sems.at[0]),
        pltpu.make_async_copy(depths_from, depths, small_sems.at[1]),
        pltpu.make_async_copy(tables_from.at[0], sigma, small_sems.at[2]),
        pltpu.make_async_copy(sums_from, sums, small_sems.at[3]),
    ]
    for copy in small:
        copy.start()
    for j in range(steps):
        copy_in(j).start()
    staged[...] = jnp.zeros(staged.shape, jnp.float32)
    for copy in small:
        copy.wait()

    total = jnp.int32(0)
    for blk in range(BLOCKS):
        total = total + flags[blk % 4, blk // 4]
    found, dry = jnp.int32(0), total
    for blk in range(BLOCKS):
        flag = flags[blk % 4, blk // 4]
        ids[jnp.where(flag > 0, found, dry)] = blk
        found = found + flag
        dry = dry + 1 - flag
    for slot in range(SLOTS):
        here = sums[pl.ds(slot, 1), :]
        mean_sigma = (here + EPSILON) / (sums[pl.ds(SLOTS + slot, 1), :] + EPSILON)
        ratio = (here + EPSILON) / (sums[pl.ds(2 * SLOTS + slot, 1), :] + EPSILON)
        mean_wavenum = ratio * ratio
        steep = here * mean_wavenum * mean_wavenum * (1.0 / STEEP_REF)
        rate = (SOURCE_STEP * DECAY_COEF) * mean_sigma / mean_wavenum * (steep * steep)
        depth = jnp.broadcast_to(depths[pl.ds(ids[slot], 1), :], (8, LANES))
        at_sea = jnp.where(slot < total, 1.0, 0.0)
        for p in range(PHASES):
            wavenum = wave_number(sigma[p] * sigma[p], depth)
            brake[p, slot] = at_sea / (1.0 + rate * wavenum)

    def step(j, carry):
        if BUFFERS < steps:

            @pl.when(j >= BUFFERS)
            def _():
                copy_out(j - BUFFERS).wait()

        copy_in(j).wait()
        here = lax.rem(j, BUFFERS)
        for q in range(PHASES):
            for slot in range(SLOTS):
                row = pl.multiple_of(j * span_in + (q * SLOTS + slot) * 8, 8)
                place = pl.ds(q * GROUP_ROWS + ids[slot], 8, stride=BLOCKS)
                staged[here, place, :] = loaded[pl.ds(row, 8), :] * brake[q, slot]
        copy_out(j).start()
        return carry

    lax.fori_loop(0, steps, step, 0)
    for j in range(steps - BUFFERS, steps):
        copy_out(j).wait()


def relax(packed, sums, depth, flags, tables):
    hbm = pl.BlockSpec(memory_space=pl.ANY)
    f32 = jnp.float32
    return pl.pallas_call(
        relax_kernel,
        out_shape=jax.ShapeDtypeStruct((GROUPS * GROUP_ROWS, LANES), f32),
        in_specs=[hbm] * 5,
        out_specs=hbm,
        scratch_shapes=[
            pltpu.VMEM((GROUPS * PACK_ROWS, LANES), f32),
            pltpu.VMEM((3 * SLOTS, LANES), f32),
            pltpu.VMEM((BLOCKS, LANES), f32),
            pltpu.SMEM((4, 4), jnp.int32),
            pltpu.VMEM((PHASES, 8, LANES), f32),
            pltpu.SMEM((BLOCKS,), jnp.int32),
            pltpu.VMEM((PHASES, SLOTS, 8, LANES), f32),
            pltpu.VMEM((BUFFERS, PHASES * GROUP_ROWS, LANES), f32),
            pltpu.SemaphoreType.DMA((4,)),
            pltpu.SemaphoreType.DMA((GROUPS // PHASES,)),
            pltpu.SemaphoreType.DMA((BUFFERS,)),
        ],
        compiler_params=pltpu.CompilerParams(vmem_limit_bytes=56 * 1024 * 1024),
        cost_estimate=pl.CostEstimate(flops=1_000_000, bytes_accessed=8_000_000, transcendentals=10_000),
    )(packed, sums, depth, flags, tables)


def tile_rows(array):
    split = array.reshape(array.shape[:-1] + (4, LANES))
    return jnp.swapaxes(split, -3, -2).reshape(-1, LANES)


def on_device(lines, spectrum, current, depth, wind, sea_blocks):
    angle = np.arange(ND + 1) * (2.0 * math.pi / ND)
    trig = jnp.asarray(np.stack([np.cos(angle), np.sin(angle)]).astype(np.float32))
    tables = jnp.asarray(phase_tables())
    depth_rows = tile_rows(depth)
    packed, sums = move(
        lines, tile_rows(spectrum), tile_rows(current), depth_rows, tile_rows(wind), sea_blocks, trig, tables
    )
    out = relax(packed, sums, depth_rows, sea_blocks, tables)
    return jnp.swapaxes(out.reshape(-1, 4, 4, LANES), 1, 2).reshape(spectrum.shape)


def solution(mesh):
    placed = (
        P("spec", "space", None),
        P(None, "space", None),
        P("space", None),
        P(None, "space", None),
        P("space", None),
    )
    return jax.shard_map(
        functools.partial(on_device, mesh.shape["space"] // LINE),
        mesh=mesh,
        in_specs=placed,
        out_specs=P("spec", "space", None),
        check_vma=False,
    )
```

```python
import functools
import math

import jax
import jax.numpy as jnp
import numpy as np
from jax import lax
from jax.experimental import pallas as pl
from jax.experimental.pallas import tpu as pltpu
from jax.sharding import PartitionSpec as P

MESH = pl.DeviceIdType.MESH
ND = 36
NF = 36
GRAVITY = 9.81
SIGMA_LOW = 2.0 * math.pi * 0.035
LOG_RATIO = math.log(1.1)
HALF_SPREAD = 0.5 * (1.1 - 1.0 / 1.1)
STEP_RATIO = 140.0 / 4600.0
SOURCE_STEP = 280.0
INPUT_COEF = 0.0002
DECAY_COEF = 0.002
STEEP_REF = 600.0
EPSILON = 1e-06

LINE = 4
LANES = 128
SLOTS = 8
GROUPS = 81
SLICE = 20
CHUNKS = ((0, 2), (2, 3), (5, 3), (8, 3), (11, 3), (14, 2), (16, 2), (18, 1), (19, 1), (20, 1))
LAST = len(CHUNKS) - 1
EARLY = 4
BUFFERS = 9
PHASES = 9
TILES = LINE + 2
BLOCKS = 16
GROUP_ROWS = 8 * BLOCKS
PACK_ROWS = 8 * SLOTS
ROWS = 4 * TILES


def phase_tables():
    sigma = SIGMA_LOW * np.exp(np.arange(NF, dtype=np.float64) * LOG_RATIO)
    weight = sigma * sigma * HALF_SPREAD * (2.0 * math.pi / ND)
    index = (np.arange(PHASES)[:, None] * 8 + np.arange(8)[None, :]) % NF
    table = np.stack([sigma, weight, weight / sigma])[:, index].astype(np.float32)
    return np.broadcast_to(table[..., None], table.shape + (LANES,)).copy()


def columns(x):
    return [x[:, ct * LANES : (ct + 1) * LANES] for ct in range(4)]


def each(function, *lists):
    return [function(*parts) for parts in zip(*lists)]


def wave_number(square, depth):
    return square * (1.0 / GRAVITY) / jnp.sqrt(jnp.tanh(square * depth * (1.0 / GRAVITY)))


def face_flux(v, half, near, far, slope, slope_before, slope_after):
    up = v >= 0.0
    other_slope = jnp.where(up, slope_before, slope_after)
    limited = jnp.maximum(jnp.minimum(other_slope, jnp.maximum(slope, 0.0)), jnp.minimum(slope, 0.0))
    return v * (jnp.where(up, near, far) + half * limited)


def half_of(v):
    return jnp.where(v >= 0.0, 0.5, -0.5) - 0.5 * v


def bin_trig(trig, first_bin):
    d, f = first_bin // NF, lax.rem(first_bin, NF)
    later = lax.broadcasted_iota(jnp.int32, (8, LANES), 0) >= NF - f
    return f, jnp.where(later, trig[0, d + 1], trig[0, d]), jnp.where(later, trig[1, d + 1], trig[1, d])


def move_kernel(
    lines,
    spectrum,
    current_from,
    depth_from,
    winds_from,
    flags_from,
    trig_from,
    tables_from,
    packed_out,
    sums_out,
    winds,
    flags,
    trig,
    tables,
    fields,
    ids,
    ids_here,
    arrived,
    field_in,
    ids_in,
    ids_near,
    cg,
    cg_rows,
    cg_cols,
    cur_rows,
    cur_cols,
    cur_left,
    sea,
    row_v,
    row_half,
    col_v,
    col_half,
    left_v,
    left_half,
    moved,
    done,
    packed,
    returned,
    root,
    number,
    gusts,
    sums_mine,
    sums_other,
    in_send,
    in_recv,
    halo_send,
    halo_recv,
    back_send,
    back_recv,
    field_send,
    field_recv,
    fhalo_send,
    fhalo_recv,
    ids_send,
    ids_recv,
    sum_send,
    sum_recv,
    keep_sem,
    small_sem,
    local_sem,
):
    space = lax.axis_index("space")
    half = lax.axis_index("spec")
    other = 1 - half
    line = space // LINE
    place = lax.rem(space, LINE)
    above = (lax.rem(line + lines - 1, lines) * LINE + place, half)
    below = (lax.rem(line + 1, lines) * LINE + place, half)
    members = [(line * LINE + s, other) for s in range(LINE)]
    longer = place == LINE - 1

    barrier = pltpu.get_barrier_semaphore()
    for peer in members + [above, below]:
        pl.semaphore_signal(barrier, inc=1, device_id=peer, device_id_type=MESH)

    small = [
        pltpu.make_async_copy(flags_from, flags, small_sem.at[0]),
        pltpu.make_async_copy(current_from, fields.at[pl.ds(0, 2 * BLOCKS)], small_sem.at[1]),
        pltpu.make_async_copy(depth_from, fields.at[pl.ds(2 * BLOCKS, BLOCKS)], small_sem.at[2]),
        pltpu.make_async_copy(tables_from, tables, small_sem.at[3]),
        pltpu.make_async_copy(winds_from, winds, small_sem.at[4]),
        pltpu.make_async_copy(trig_from, trig, small_sem.at[5]),
    ]
    for copy in small:
        copy.start()
    for copy in small:
        copy.wait()

    lane = lax.broadcasted_iota(jnp.int32, (8, LANES), 1)
    numbers = jnp.zeros((8, LANES), jnp.int32)
    found = jnp.int32(0)
    for blk in range(BLOCKS):
        flag = flags[blk % 4, blk // 4]
        fields[3 * BLOCKS + blk : 3 * BLOCKS + blk + 1] = jnp.full((1, LANES), flag.astype(jnp.float32))
        numbers = jnp.where(lane == jnp.where(flag > 0, found, -1), blk, numbers)
        found = found + flag
    ids[...] = numbers
    pl.semaphore_wait(barrier, LINE + 2)

    def remote(src, dst, send, recv, device):
        return pltpu.make_async_remote_copy(
            src_ref=src, dst_ref=dst, send_sem=send, recv_sem=recv, device_id=device, device_id_type=MESH
        )

    def into(c, s, sender):
        first, count = CHUNKS[c]
        return remote(
            spectrum.at[pl.ds((SLICE * s + first) * GROUP_ROWS, count * GROUP_ROWS)],
            arrived.at[1 + sender, pl.ds(first * GROUP_ROWS, count * GROUP_ROWS)],
            in_send.at[c, s],
            in_recv.at[c, sender],
            members[s],
        )

    def halo(c, down):
        first, count = CHUNKS[c]
        part = pl.ds(first * GROUP_ROWS, count * GROUP_ROWS)
        tile, target, device = (LINE, 0, below) if down else (1, LINE + 1, above)
        side = 0 if down else 1
        return remote(
            arrived.at[tile, part], arrived.at[target, part], halo_send.at[c, side], halo_recv.at[c, side], device
        )

    def back(c, i, sender):
        first, count = CHUNKS[c]
        start = pl.multiple_of((SLICE * sender + first) * PACK_ROWS, 8)
        return remote(
            packed.at[i, pl.ds(first * PACK_ROWS, count * PACK_ROWS)],
            returned.at[pl.ds(start, count * PACK_ROWS)],
            back_send.at[c, i],
            back_recv.at[c, sender],
            members[i],
        )

    def field_into(s, sender):
        return remote(fields, field_in.at[1 + sender], field_send.at[s], field_recv.at[sender], members[s])

    def ids_into(s, sender):
        return remote(ids, ids_in.at[sender], ids_send.at[s], ids_recv.at[sender], members[s])

    def field_halo(down):
        tile, target, device = (LINE, 0, below) if down else (1, LINE + 1, above)
        side = 0 if down else 1
        return remote(field_in.at[tile], field_in.at[target], fhalo_send.at[side], fhalo_recv.at[side], device)

    def slices(c):
        return range(LINE) if c < LAST else (LINE - 1,)

    def send_in(c):
        for s in slices(c):
            into(c, s, place).start()

    for s in range(LINE):
        field_into(s, place).start()
    for s in range(LINE):
        ids_into(s, place).start()
    for c in range(EARLY):
        send_in(c)
    send_in(LAST)
    for c in range(EARLY, LAST):
        send_in(c)

    ids_copy = pltpu.make_async_copy(ids, ids_here, local_sem)
    ids_copy.start()
    ids_copy.wait()

    def root_phase(p, carry):
        square = tables[0, p] * tables[0, p]
        for slot in range(SLOTS):
            depth = fields[pl.ds(2 * BLOCKS + ids_here[0, slot], 1), :]
            wavenum = wave_number(square, jnp.broadcast_to(depth, (8, LANES)))
            root[p, slot] = tables[1, p] / jnp.sqrt(wavenum)
            number[p, slot] = wavenum * (SOURCE_STEP * INPUT_COEF)
        return carry

    for slot in range(SLOTS):
        for part in range(2):
            wind = winds[pl.ds(part * BLOCKS + ids_here[0, slot], 1), :]
            gusts[part, slot] = jnp.broadcast_to(wind, (8, LANES))

    lax.fori_loop(0, PHASES, root_phase, 0)

    for i in range(LINE):
        field_into(i, i).wait_recv()
    field_halo(True).start()
    field_halo(False).start()
    for i in range(LINE):
        ids_into(i, i).wait_recv()
    near_copy = pltpu.make_async_copy(ids_in, ids_near, local_sem)
    near_copy.start()
    near_copy.wait()
    field_halo(True).wait_recv()
    field_halo(False).wait_recv()

    first_line = jnp.where(line == 0, 0.0, 1.0)
    last_line = jnp.where(line == lines - 1, 0.0, 1.0)
    at_start = lane == 0
    at_end = lane == LANES - 1

    def shift_left(parts):
        turned = [pltpu.roll(part, LANES - 1, 1) for part in parts] + [jnp.zeros((8, LANES), jnp.float32)]
        return [jnp.where(at_end, turned[ct + 1], turned[ct]) for ct in range(4)]

    def shift_right(parts, first):
        turned = [first] + [pltpu.roll(part, 1, 1) for part in parts]
        return [jnp.where(at_start, turned[ct], turned[ct + 1]) for ct in range(4)]

    def table_row(row, carry):
        tile, r = row // 4, lax.rem(row, 4)
        kept = jnp.where(tile == 0, first_line, jnp.where(tile == LINE + 1, last_line, 1.0))
        scale = 0.5 * STEP_RATIO * kept

        def field_row(which, ct):
            return jnp.broadcast_to(field_in[tile, pl.ds(which * BLOCKS + ct * 4 + r, 1), :], (8, LANES))

        across = [field_row(1, ct) * scale for ct in range(4)]
        cur_left[row] = across[0]
        faces = each(jnp.add, across, shift_left(across))
        for ct in range(4):
            cur_rows[row, ct] = field_row(0, ct) * scale
            cur_cols[row, ct] = faces[ct]
            sea[row, ct] = field_row(3, ct) * kept
        depths = [field_row(2, ct) for ct in range(4)]
        for p in range(5):
            sig = tables[0, p]
            speeds = []
            for ct in range(4):
                wavenum = wave_number(sig * sig, depths[ct])
                product = wavenum * depths[ct]
                damping = jnp.exp(-2.0 * product)
                shallow = 4.0 * product * damping / (1.0 - damping * damping)
                speeds.append((0.5 * scale) * (sig / wavenum) * (1.0 + shallow))
            faces = each(jnp.add, speeds, shift_left(speeds))
            for ct in range(4):
                cg[row, ct, 8 * p : 8 * p + 8] = speeds[ct]
                cg_cols[row, ct, 8 * p : 8 * p + 8] = faces[ct]
        return carry

    def face_row(row, carry):
        cg_rows[row] = cg[row] + cg[row + 1]
        cur_rows[row] = cur_rows[row] + cur_rows[row + 1]
        return carry

    def take_in(c):
        for i in range(LINE):
            into(c, i if c < LAST else LINE - 1, i).wait_recv()
        halo(c, True).start()
        halo(c, False).start()

    lax.fori_loop(0, ROWS // 2, table_row, 0)
    take_in(0)
    lax.fori_loop(ROWS // 2, ROWS, table_row, 0)
    lax.fori_loop(0, ROWS - 1, face_row, 0)

    def advance(load, store, first, tiles, row_speed, col_speed, last_mask):
        rows = [load(first - 2 + j) for j in range(4)]
        slopes = [each(jnp.subtract, rows[j + 1], rows[j]) for j in range(3)]
        flux = each(face_flux, *row_speed(first - 1), rows[1], rows[2], slopes[1], slopes[0], slopes[2])

        def body(t, carry):
            near, far, slope_before, slope, flux_before = carry
            for r in range(4):
                row = first + 4 * t + r
                after = load(row + 2)
                slope_after = each(jnp.subtract, after, far)
                flux = each(face_flux, *row_speed(row), near, far, slope, slope_before, slope_after)
                mask = [sea[row, ct] for ct in range(4)]
                x = each(lambda n, a, b, m: (n - (a - b)) * m, near, flux, flux_before, mask)
                right = shift_left(x)
                d = each(jnp.subtract, right, x)
                v, half_v, edge_v, edge_half = col_speed(row)
                across = each(face_flux, v, half_v, x, right, d, shift_right(d, x[0]), shift_left(d))
                limited = jnp.maximum(jnp.minimum(d[0], jnp.maximum(x[0], 0.0)), jnp.minimum(x[0], 0.0))
                before = shift_right(across, edge_v * (x[0] - edge_half * limited))
                out = each(lambda n, a, b: n - (a - b), x, across, before)
                store(t, r, each(jnp.multiply, out, mask) if last_mask else out)
                near, far, slope_before, slope, flux_before = far, after, slope, slope_after, flux
            return near, far, slope_before, slope, flux_before

        lax.fori_loop(0, tiles, body, (rows[2], rows[3], slopes[1], slopes[2], flux))

    def one_group(group, carry):
        for c in range(1, LAST + 1):
            if c < LAST:

                @pl.when(group == CHUNKS[c - 1][0])
                def _(c=c):
                    take_in(c)

            else:

                @pl.when((group == CHUNKS[c - 1][0]) & longer)
                def _(c=c):
                    take_in(c)

        for c in range(LAST + 1):

            @pl.when(group == CHUNKS[c][0])
            def _(c=c):
                halo(c, True).wait_recv()
                halo(c, False).wait_recv()
                first, count = CHUNKS[c]
                zeros = jnp.zeros((GROUP_ROWS, LANES), jnp.float32)

                @pl.when(line == 0)
                def _():
                    for q in range(count):
                        arrived[0, pl.ds((first + q) * GROUP_ROWS, GROUP_ROWS)] = zeros

                @pl.when(line == lines - 1)
                def _():
                    for q in range(count):
                        arrived[LINE + 1, pl.ds((first + q) * GROUP_ROWS, GROUP_ROWS)] = zeros

        f, cosine, sine = bin_trig(trig, other * (8 * GROUPS) + 8 * (SLICE * place + group))

        def load_first(row):
            tile, r = row // 4, lax.rem(row, 4)
            return [
                arrived[tile, pl.ds(group * GROUP_ROWS + ct * 4 + r, 8, stride=BLOCKS), :] for ct in range(4)
            ]

        def store_first(t, r, value):
            for ct in range(4):
                moved[2 + 4 * t + r, ct] = value[ct]

        def load_second(row):
            return [moved[row, ct] for ct in range(4)]

        def store_second(t, r, value):
            for ct in range(4):
                done[t * BLOCKS + ct * 4 + r] = value[ct]

        def row_first(row):
            v = [cg_rows[row, ct, pl.ds(f, 8), :] * cosine + cur_rows[row, ct] for ct in range(4)]
            halves = each(half_of, v)
            for ct in range(4):
                row_v[row, ct] = v[ct]
                row_half[row, ct] = halves[ct]
            return v, halves

        def col_first(row):
            v = [cg_cols[row, ct, pl.ds(f, 8), :] * sine + cur_cols[row, ct] for ct in range(4)]
            halves = each(half_of, v)
            for ct in range(4):
                col_v[row, ct] = v[ct]
                col_half[row, ct] = halves[ct]
            edge = cg[row, 0, pl.ds(f, 8), :] * sine + cur_left[row]
            edge_v, edge_half = jnp.minimum(edge, 0.0), 0.5 + 0.5 * edge
            left_v[row] = edge_v
            left_half[row] = edge_half
            return v, halves, edge_v, edge_half

        def row_again(row):
            return [row_v[row, ct] for ct in range(4)], [row_half[row, ct] for ct in range(4)]

        def col_again(row):
            v, halves = [col_v[row, ct] for ct in range(4)], [col_half[row, ct] for ct in range(4)]
            return v, halves, left_v[row], left_half[row]

        advance(load_first, store_first, 2, LINE + 1, row_first, col_first, True)
        advance(load_second, store_second, 4, LINE, row_again, col_again, False)
        for i in range(LINE):
            for slot in range(SLOTS):
                start = pl.multiple_of((group * SLOTS + slot) * 8, 8)
                packed[i, pl.ds(start, 8), :] = done[i * BLOCKS + ids_near[i, 0, slot]]

        for c in range(LAST + 1):

            @pl.when(group == CHUNKS[c][0] + CHUNKS[c][1] - 1)
            def _(c=c):
                for i in range(LINE):
                    back(c, i, place).start()

        return carry

    lax.fori_loop(0, jnp.where(longer, SLICE + 1, SLICE), one_group, 0)

    for s in range(LINE):
        field_into(s, place).wait_send()
        ids_into(s, place).wait_send()
    field_halo(True).wait_send()
    field_halo(False).wait_send()
    for c in range(LAST + 1):
        for s in slices(c):
            into(c, s, place).wait_send()

    split = CHUNKS[LAST - 2][0]

    def keep(late, s):
        begin, end = (split, SLICE + (s == LINE - 1)) if late else (0, split)
        part = pl.ds((SLICE * s + begin) * PACK_ROWS, (end - begin) * PACK_ROWS)
        return pltpu.make_async_copy(returned.at[part], packed_out.at[part], keep_sem.at[late, s])

    totals = (jnp.zeros((8, LANES), jnp.float32),) * (3 * SLOTS)
    for c in range(LAST + 1):
        for s in slices(c):
            back(c, s, s).wait_recv()

        def add(m, carry, c=c):
            result = list(carry)
            for s in slices(c):
                g = SLICE * s + m
                phase = lax.rem(g, PHASES)
                weight, over = tables[1, phase], tables[2, phase]
                gain = tables[0, phase] * (SOURCE_STEP * INPUT_COEF)
                _, cosine, sine = bin_trig(trig, half * (8 * GROUPS) + 8 * g)
                for slot in range(SLOTS):
                    start = pl.multiple_of((g * SLOTS + slot) * 8, 8)
                    value = returned[pl.ds(start, 8), :]
                    result[slot] += value * weight
                    result[SLOTS + slot] += value * over
                    result[2 * SLOTS + slot] += value * root[phase, slot]
                    along = gusts[0, slot] * cosine + gusts[1, slot] * sine
                    growth = jnp.maximum(along * number[phase, slot] - gain, 0.0)
                    returned[pl.ds(start, 8), :] = value * (1.0 + growth)
            return tuple(result)

        first, count = CHUNKS[c]
        totals = lax.fori_loop(first, first + count, add, totals)
        if c == LAST - 3:
            for s in range(LINE):
                keep(0, s).start()
    for s in range(LINE):
        keep(1, s).start()
    for q in range(3 * SLOTS):
        sums_mine[pl.ds(q, 1), :] = jnp.sum(totals[q], axis=0, keepdims=True)
    swap = remote(sums_mine, sums_other, sum_send, sum_recv, (space, other))
    swap.start()

    for c in range(LAST):
        halo(c, True).wait_send()
        halo(c, False).wait_send()
        for i in range(LINE):
            back(c, i, place).wait_send()

    @pl.when(longer)
    def _():
        halo(LAST, True).wait_send()
        halo(LAST, False).wait_send()
        for i in range(LINE):
            back(LAST, i, place).wait_send()

    for s in range(LINE):
        keep(0, s).wait()
        keep(1, s).wait()
    swap.wait()
    sums_out[...] = sums_mine[...] + sums_other[...]


def move(lines, spectrum, current, depth, wind, flags, trig, tables):
    vmem = pl.BlockSpec(memory_space=pltpu.VMEM)
    hbm = pl.BlockSpec(memory_space=pl.ANY)
    f32 = jnp.float32
    dma = pltpu.SemaphoreType.DMA
    parts = len(CHUNKS)

    def tiles(*shape):
        return pltpu.VMEM(shape + (8, LANES), f32)

    return pl.pallas_call(
        functools.partial(move_kernel, lines),
        out_shape=(
            jax.ShapeDtypeStruct((GROUPS * PACK_ROWS, LANES), f32),
            jax.ShapeDtypeStruct((3 * SLOTS, LANES), f32),
        ),
        in_specs=[hbm] * 7,
        out_specs=(hbm, vmem),
        scratch_shapes=[
            pltpu.VMEM((2 * BLOCKS, LANES), f32),
            pltpu.SMEM((4, 4), jnp.int32),
            pltpu.SMEM((2, ND + 1), f32),
            tiles(3, PHASES),
            pltpu.VMEM((4 * BLOCKS, LANES), f32),
            pltpu.VMEM((8, LANES), jnp.int32),
            pltpu.SMEM((8, LANES), jnp.int32),
            pltpu.VMEM((TILES, (SLICE + 1) * GROUP_ROWS, LANES), f32),
            pltpu.VMEM((TILES, 4 * BLOCKS, LANES), f32),
            pltpu.VMEM((LINE, 8, LANES), jnp.int32),
            pltpu.SMEM((LINE, 8, LANES), jnp.int32),
            pltpu.VMEM((ROWS, 4, 40, LANES), f32),
            pltpu.VMEM((ROWS, 4, 40, LANES), f32),
            pltpu.VMEM((ROWS, 4, 40, LANES), f32),
            tiles(ROWS, 4),
            tiles(ROWS, 4),
            tiles(ROWS),
            tiles(ROWS, 4),
            tiles(ROWS, 4),
            tiles(ROWS, 4),
            tiles(ROWS, 4),
            tiles(ROWS, 4),
            tiles(ROWS),
            tiles(ROWS),
            tiles(ROWS, 4),
            tiles(LINE * BLOCKS),
            pltpu.VMEM((LINE, (SLICE + 1) * PACK_ROWS, LANES), f32),
            pltpu.VMEM((GROUPS * PACK_ROWS, LANES), f32),
            tiles(PHASES, SLOTS),
            tiles(PHASES, SLOTS),
            tiles(2, SLOTS),
            pltpu.VMEM((3 * SLOTS, LANES), f32),
            pltpu.VMEM((3 * SLOTS, LANES), f32),
            dma((parts, LINE)),
            dma((parts, LINE)),
            dma((parts, 2)),
            dma((parts, 2)),
            dma((parts, LINE)),
            dma((parts, LINE)),
            dma((LINE,)),
            dma((LINE,)),
            dma((2,)),
            dma((2,)),
            dma((LINE,)),
            dma((LINE,)),
            dma,
            dma,
            dma((2, LINE)),
            dma((6,)),
            dma,
        ],
        compiler_params=pltpu.CompilerParams(
            collective_id=0, has_side_effects=True, vmem_limit_bytes=56 * 1024 * 1024
        ),
        cost_estimate=pl.CostEstimate(flops=250_000_000, bytes_accessed=16_000_000, transcendentals=1_000_000),
    )(spectrum, current, depth, wind, flags, trig, tables)


def relax_kernel(
    packed,
    sums_from,
    depths_from,
    flags_from,
    tables_from,
    out,
    loaded,
    sums,
    depths,
    flags,
    sigma,
    ids,
    brake,
    staged,
    small_sems,
    in_sems,
    out_sems,
):
    span_in, span_out = PHASES * PACK_ROWS, PHASES * GROUP_ROWS
    steps = GROUPS // PHASES

    def copy_in(j):
        part = pl.ds(pl.multiple_of(j * span_in, 8), span_in)
        return pltpu.make_async_copy(packed.at[part], loaded.at[part], in_sems.at[j])

    def copy_out(j):
        here = lax.rem(j, BUFFERS)
        part = pl.ds(pl.multiple_of(j * span_out, 8), span_out)
        return pltpu.make_async_copy(staged.at[here], out.at[part], out_sems.at[here])

    small = [
        pltpu.make_async_copy(flags_from, flags, small_sems.at[0]),
        pltpu.make_async_copy(depths_from, depths, small_sems.at[1]),
        pltpu.make_async_copy(tables_from.at[0], sigma, small_sems.at[2]),
        pltpu.make_async_copy(sums_from, sums, small_sems.at[3]),
    ]
    for copy in small:
        copy.start()
    for j in range(steps):
        copy_in(j).start()
    staged[...] = jnp.zeros(staged.shape, jnp.float32)
    for copy in small:
        copy.wait()

    total = jnp.int32(0)
    for blk in range(BLOCKS):
        total = total + flags[blk % 4, blk // 4]
    found, dry = jnp.int32(0), total
    for blk in range(BLOCKS):
        flag = flags[blk % 4, blk // 4]
        ids[jnp.where(flag > 0, found, dry)] = blk
        found = found + flag
        dry = dry + 1 - flag
    for slot in range(SLOTS):
        here = sums[pl.ds(slot, 1), :]
        mean_sigma = (here + EPSILON) / (sums[pl.ds(SLOTS + slot, 1), :] + EPSILON)
        ratio = (here + EPSILON) / (sums[pl.ds(2 * SLOTS + slot, 1), :] + EPSILON)
        mean_wavenum = ratio * ratio
        steep = here * mean_wavenum * mean_wavenum * (1.0 / STEEP_REF)
        rate = (SOURCE_STEP * DECAY_COEF) * mean_sigma / mean_wavenum * (steep * steep)
        depth = jnp.broadcast_to(depths[pl.ds(ids[slot], 1), :], (8, LANES))
        at_sea = jnp.where(slot < total, 1.0, 0.0)
        for p in range(PHASES):
            wavenum = wave_number(sigma[p] * sigma[p], depth)
            brake[p, slot] = at_sea / (1.0 + rate * wavenum)

    def step(j, carry):
        if BUFFERS < steps:

            @pl.when(j >= BUFFERS)
            def _():
                copy_out(j - BUFFERS).wait()

        copy_in(j).wait()
        here = lax.rem(j, BUFFERS)
        for q in range(PHASES):
            for slot in range(SLOTS):
                row = pl.multiple_of(j * span_in + (q * SLOTS + slot) * 8, 8)
                place = pl.ds(q * GROUP_ROWS + ids[slot], 8, stride=BLOCKS)
                staged[here, place, :] = loaded[pl.ds(row, 8), :] * brake[q, slot]
        copy_out(j).start()
        return carry

    lax.fori_loop(0, steps, step, 0)
    for j in range(steps - BUFFERS, steps):
        copy_out(j).wait()


def relax(packed, sums, depth, flags, tables):
    hbm = pl.BlockSpec(memory_space=pl.ANY)
    f32 = jnp.float32
    return pl.pallas_call(
        relax_kernel,
        out_shape=jax.ShapeDtypeStruct((GROUPS * GROUP_ROWS, LANES), f32),
        in_specs=[hbm] * 5,
        out_specs=hbm,
        scratch_shapes=[
            pltpu.VMEM((GROUPS * PACK_ROWS, LANES), f32),
            pltpu.VMEM((3 * SLOTS, LANES), f32),
            pltpu.VMEM((BLOCKS, LANES), f32),
            pltpu.SMEM((4, 4), jnp.int32),
            pltpu.VMEM((PHASES, 8, LANES), f32),
            pltpu.SMEM((BLOCKS,), jnp.int32),
            pltpu.VMEM((PHASES, SLOTS, 8, LANES), f32),
            pltpu.VMEM((BUFFERS, PHASES * GROUP_ROWS, LANES), f32),
            pltpu.SemaphoreType.DMA((4,)),
            pltpu.SemaphoreType.DMA((GROUPS // PHASES,)),
            pltpu.SemaphoreType.DMA((BUFFERS,)),
        ],
        compiler_params=pltpu.CompilerParams(vmem_limit_bytes=56 * 1024 * 1024),
        cost_estimate=pl.CostEstimate(flops=1_000_000, bytes_accessed=8_000_000, transcendentals=10_000),
    )(packed, sums, depth, flags, tables)


def tile_rows(array):
    split = array.reshape(array.shape[:-1] + (4, LANES))
    return jnp.swapaxes(split, -3, -2).reshape(-1, LANES)


def on_device(lines, spectrum, current, depth, wind, sea_blocks):
    angle = np.arange(ND + 1) * (2.0 * math.pi / ND)
    trig = jnp.asarray(np.stack([np.cos(angle), np.sin(angle)]).astype(np.float32))
    tables = jnp.asarray(phase_tables())
    depth_rows = tile_rows(depth)
    packed, sums = move(
        lines, tile_rows(spectrum), tile_rows(current), depth_rows, tile_rows(wind), sea_blocks, trig, tables
    )
    out = relax(packed, sums, depth_rows, sea_blocks, tables)
    return jnp.swapaxes(out.reshape(-1, 4, 4, LANES), 1, 2).reshape(spectrum.shape)


def solution(mesh):
    placed = (
        P("spec", "space", None),
        P(None, "space", None),
        P("space", None),
        P(None, "space", None),
        P("space", None),
    )
    return jax.shard_map(
        functools.partial(on_device, mesh.shape["space"] // LINE),
        mesh=mesh,
        in_specs=placed,
        out_specs=P("spec", "space", None),
        check_vma=False,
    )
```
